32 devices in a mesh: grp: 2 (over x), seq: 8 (over z, y), tp: 2 (over core).
Axes of the slice: x: 2, y: 2, z: 4, core: 2. Of those that a mesh axis runs over, the one named last changes fastest.
Arguments:
- queries: bfloat16 [16384, 1536], P(('grp', 'seq'), 'tp'), parts along dimension 0, may hold values from -6 to 6
- attn_keys: bfloat16 [16384, 1536], P(('grp', 'seq'), 'tp'), parts along dimension 0, may hold values from -6 to 6
- attn_values: bfloat16 [16384, 1536], P(('grp', 'seq'), 'tp'), parts along dimension 0, may hold values from -6 to 6
- out_weight: bfloat16 [1536, 3072], P('tp'), may hold values from -0.15625 to 0.15625
- residual: bfloat16 [16384, 3072], P(('grp', 'seq'), 'tp'), parts along dimension 0, may hold values from -40 to 40
- norm_gain: float32 [3072], P('tp'), may hold values from 0.1 to 1.9
- conv_weight: float32 [31, 3072], P(None, 'tp'), may hold values from -1 to 1
- record_starts: int32 [16], P('grp'), parts along dimension 0, may hold values from 0 to 7039, as said below
- record_lengths: int32 [16], P('grp'), parts along dimension 0, may hold values from 256 to 1153, as said below
Outputs:
- block_out: bfloat16 [16384, 3072], P(('grp', 'seq'), 'tp'), parts along dimension 0
The draws below stay inside these ranges and needn't reach their ends.
There are 2 independent parts, one for each index of `grp`. The reference program is written for one: setup_inputs(seed, part) draws one part's arguments, and reference() takes and returns one part's arrays. A program takes and returns all parts, laid end to end along the dimension named above; an argument that names none is the same for every part. Nothing has to cross between parts.
Inputs may be any that keep to these rules, and one draw needn't show every extreme that they name: `record_starts`: recording r lies in its stretch: frames 0 to 511 for r = 0; frames r * 1024 - 1024 // 2 to (r + 1) * 1024 - 1024 // 2 - 1 for 0 < r < 7; frames (7) * 1024 - 1024 // 2 to 8191 for the last. It starts within the first quarter of its stretch; recording 0 starts at frame 0. `record_lengths`: each recording ends inside its stretch.
All inputs are finite; a program needn't handle non-finite values.
Results may differ from the reference program's by a relative error of at most 0.0025.
Values may be sent and summed in bfloat16 or wider, within the bound.
No kernel may reach another device: no remote copies, remote signals or barrier semaphores. Data moves between devices by JAX's collectives and lax.ppermute only.
A program may use at most 128 MiB of HBM per device.

```python
import jax
import jax.numpy as jnp
from jax import lax

D = 3072
HSIZE = 64
WIN = 128
KHALF = 15
REC = 8
TOK_DEV = 1024
HD = 1536
KERNEL = 31
TOKENS = 8192
SLOT = 1024


def query_key_pair(key):
    query_base = jnp.clip(jax.random.normal(jax.random.fold_in(key, 11), (TOKENS, HD), jnp.float32), -4.5, 4.5)
    key_base = jnp.clip(jax.random.normal(jax.random.fold_in(key, 12), (TOKENS, HD), jnp.float32), -4.5, 4.5)
    return (query_base, key_base)


def draw_queries(key, part):
    return query_key_pair(key)[0].astype(jnp.bfloat16)


def draw_attn_keys(key, part):
    return query_key_pair(key)[1].astype(jnp.bfloat16)


def draw_residual(key, part):
    row_scale = jnp.exp(jax.random.uniform(jax.random.fold_in(key, 41), (TOKENS, 1), jnp.float32, jnp.log(0.3), jnp.log(3.0)))
    column_scale = jnp.exp(jax.random.uniform(jax.random.fold_in(key, 42), (1, D), jnp.float32, jnp.log(0.3), jnp.log(3.0)))
    values_base = jnp.clip(jax.random.normal(jax.random.fold_in(key, 45), (TOKENS, D), jnp.float32), -4.0, 4.0)
    return (values_base * row_scale * column_scale).astype(jnp.bfloat16)


def record_layout(key):
    record_index = jnp.arange(REC, dtype=jnp.int32)
    stretch_start = jnp.where(record_index == 0, 0, record_index * SLOT - SLOT // 2)
    stretch_size = jnp.where(record_index == 0, SLOT // 2, jnp.where(record_index == REC - 1, SLOT + SLOT // 2, SLOT))
    quarter = stretch_size // 4
    gap_frames = jax.random.randint(jax.random.fold_in(key, 32), (REC,), 0, quarter)
    gap_frames = jnp.where(record_index == REC - 1, quarter - 1, gap_frames)
    gap_frames = jnp.where((record_index == 0) | (record_index == REC // 2), 0, gap_frames)
    half_size = stretch_size // 2
    span_frames = half_size + jax.random.randint(jax.random.fold_in(key, 33), (REC,), 0, stretch_size - gap_frames - half_size + 1)
    span_frames = jnp.where(record_index == REC // 2, stretch_size, span_frames)
    span_frames = jnp.where(record_index == REC - 1, stretch_size - gap_frames, span_frames)
    span_frames = jnp.where(record_index == 0, SLOT // 4, span_frames)
    return ((stretch_start + gap_frames).astype(jnp.int32), span_frames.astype(jnp.int32))


def draw_record_starts(key, part):
    return record_layout(key)[0]


def draw_record_lengths(key, part):
    return record_layout(key)[1]


def steps_of(own_key, dims, cuts, low, top_value):
    gain, own = 1.0, jax.random.fold_in(own_key, 6)
    for position, shards_of in cuts:
        steps = jnp.exp(jax.random.uniform(jax.random.fold_in(own, position), (shards_of,), jnp.float32, low / len(cuts), top_value / len(cuts)))
        gain = gain * jnp.repeat(steps, dims[position] // shards_of).reshape([-1 if axis == position else 1 for axis in range(len(dims))])
    return gain


def noise(rng, shape, deviation, limit, split=(), kind=jnp.bfloat16):
    array = jax.random.normal(rng, shape, jnp.float32) * deviation
    if len(split) > 0:
        array = steps_of(rng, shape, split, -0.22, 0.18) * array
    return jnp.clip(array, min=-limit, max=limit).astype(kind)


def setup_inputs(seed: int = 0, part: int = 0) -> dict:
    streams_of = jax.random.split(jax.random.key(seed), 10)
    part_splits = jax.random.split(jax.random.fold_in(streams_of[9], part), 10)
    return {
        "queries": draw_queries(jax.random.fold_in(jax.random.fold_in(streams_of[9], part), 71), part),
        "attn_keys": draw_attn_keys(jax.random.fold_in(jax.random.fold_in(streams_of[9], part), 71), part),
        "attn_values": noise(part_splits[2], (TOKENS, HD), 1.0, 6.0, ((0, 8), (1, 2))),
        "out_weight": noise(streams_of[3], (HD, D), HD ** -0.5, 0.15625, ((0, 2),)),
        "residual": draw_residual(jax.random.fold_in(jax.random.fold_in(streams_of[9], part), 71), part),
        "norm_gain": jnp.clip(1.0 + 0.18 * jax.random.normal(streams_of[5], (D,), jnp.float32), 0.1, 1.9),
        "conv_weight": noise(streams_of[6], (KERNEL, D), KERNEL ** -0.5, 1.0, ((1, 2),), jnp.float32),
        "record_starts": draw_record_starts(jax.random.fold_in(jax.random.fold_in(streams_of[9], part), 71), part),
        "record_lengths": draw_record_lengths(jax.random.fold_in(jax.random.fold_in(streams_of[9], part), 71), part),
    }


def segment_of(positions, record_starts, record_lengths):
    inside = (positions[:, None] >= record_starts[None, :]) & (positions[:, None] < (record_starts + record_lengths)[None, :])
    labels = jnp.arange(1, REC + 1, dtype=jnp.int32)
    return (lax.optimization_barrier(jnp.sum(jnp.where(inside, labels[None, :], 0), axis=1)) - 1).astype(jnp.int32)

def attend(query_block, key_block, value_block, query_segment, key_segment):
    block_rows = query_block.shape[0]
    key_span = key_block.shape[0]
    head_count = query_block.shape[1] // HSIZE
    query_heads = query_block.astype(jnp.float32).reshape(block_rows, head_count, HSIZE)
    key_heads = key_block.astype(jnp.float32).reshape(key_span, head_count, HSIZE)
    value_heads = value_block.astype(jnp.float32).reshape(key_span, head_count, HSIZE)
    scores = jnp.einsum('qhd,khd->hqk', query_heads, key_heads) * HSIZE ** (-0.5)
    distance = jnp.arange(key_span)[None, :] - jnp.arange(block_rows)[:, None] - WIN
    allowed = (jnp.abs(distance) <= WIN) & (query_segment[:, None] == key_segment[None, :]) & (query_segment[:, None] >= 0)
    masked = jnp.where(allowed[None], scores, jnp.float32(-1e+30))
    row_max = lax.optimization_barrier(jnp.max(masked, axis=-1, keepdims=True))
    exponent = jnp.where(allowed[None], jnp.exp(masked - row_max), jnp.float32(0.0))
    row_total = lax.optimization_barrier(jnp.sum(exponent, axis=-1))
    divisor = jnp.where(query_segment[None, :] >= 0, row_total, jnp.float32(1.0))
    weights = lax.optimization_barrier(exponent.astype(jnp.bfloat16)).astype(jnp.float32)
    mixed_heads = jnp.einsum('hqk,khd->qhd', weights, value_heads) / jnp.transpose(divisor)[:, :, None]
    mixed_heads = jnp.where(query_segment[:, None, None] >= 0, mixed_heads, jnp.float32(0.0))
    return mixed_heads.reshape(block_rows, head_count * HSIZE).astype(jnp.bfloat16)

def reference(queries, attn_keys, attn_values, out_weight, residual, norm_gain, conv_weight, record_starts, record_lengths):
    frames = queries.shape[0]
    positions = jnp.arange(frames, dtype=jnp.int32)
    segment = segment_of(positions, record_starts, record_lengths)
    valid = segment >= 0
    block_rows = min(256, TOK_DEV)
    padded_keys = jnp.pad(attn_keys, ((WIN, WIN), (0, 0)))
    padded_values = jnp.pad(attn_values, ((WIN, WIN), (0, 0)))
    padded_segment = jnp.pad(segment, (WIN, WIN), constant_values=-1).astype(jnp.int32)

    def one_block(block_id):
        block_start = (block_id * block_rows).astype(jnp.int32)
        query_block = lax.dynamic_slice_in_dim(queries, block_start, block_rows, 0)
        key_block = lax.dynamic_slice_in_dim(padded_keys, block_start, block_rows + 2 * WIN, 0)
        value_block = lax.dynamic_slice_in_dim(padded_values, block_start, block_rows + 2 * WIN, 0)
        query_segment = lax.dynamic_slice_in_dim(segment, block_start, block_rows, 0)
        key_segment = lax.dynamic_slice_in_dim(padded_segment, block_start, block_rows + 2 * WIN, 0)
        return attend(query_block, key_block, value_block, query_segment, key_segment)
    blocks = lax.map(one_block, jnp.arange(frames // block_rows, dtype=jnp.int32))
    attended = blocks.reshape(frames, -1)
    projected = jnp.dot(attended, out_weight, preferred_element_type=jnp.float32)
    hidden_sum = residual.astype(jnp.float32) + projected
    row_mean = lax.optimization_barrier(jnp.mean(hidden_sum, axis=1, keepdims=True))
    centered = hidden_sum - row_mean
    row_var = lax.optimization_barrier(jnp.mean(centered * centered, axis=1, keepdims=True))
    normed = centered * lax.rsqrt(row_var + jnp.float32(1e-05)) * norm_gain[None, :]
    normed = jnp.where(valid[:, None], normed, jnp.float32(0.0)).astype(jnp.bfloat16)
    padded_normed = jnp.pad(normed, ((KHALF, KHALF), (0, 0)))
    normed_segment = jnp.pad(segment, (KHALF, KHALF), constant_values=-1).astype(jnp.int32)
    conv_sum = jnp.zeros(hidden_sum.shape, jnp.float32)
    for tap_index in range(KERNEL):
        shifted = padded_normed[tap_index:tap_index + frames].astype(jnp.float32)
        same_record = normed_segment[tap_index:tap_index + frames] == segment
        conv_sum = conv_sum + jnp.where(same_record[:, None], conv_weight[tap_index][None, :] * shifted, jnp.float32(0.0))
    return (hidden_sum + jax.nn.silu(conv_sum)).astype(jnp.bfloat16)
```

```python
import functools

import jax
import jax.numpy as jnp
from jax import lax
from jax.experimental import pallas as pl
from jax.experimental.pallas import tpu as pltpu
from jax.sharding import PartitionSpec as P

D = 3072
HSIZE = 64
WIN = 128
KHALF = 15
REC = 8
KERNEL = 31
EDGE = 16
REACH = WIN + EDGE
SPAN = 512
LANES = 128
NEG = -1e30
EXP_SCALE = HSIZE ** (-0.5) * 1.4426950408889634
SMEM = pl.BlockSpec(memory_space=pltpu.SMEM)


def row_bounds(positions, starts_ref, lengths_ref):
    first = jnp.full(positions.shape, -1, jnp.int32)
    last = jnp.full(positions.shape, -2, jnp.int32)
    for r in range(REC):
        start = starts_ref[r]
        end = start + lengths_ref[r]
        inside = (positions >= start) & (positions < end)
        first = jnp.where(inside, start, first)
        last = jnp.where(inside, end - 1, last)
    return first, last


def as_column(row):
    return jnp.transpose(jnp.broadcast_to(row, (LANES, LANES)))


def band_bias(base, rows, key_base, keys, starts_ref, lengths_ref, store):
    for top in range(0, rows, LANES):
        count = min(LANES, rows - top)
        positions = base + top + lax.broadcasted_iota(jnp.int32, (1, LANES), 1)
        first, last = row_bounds(positions, starts_ref, lengths_ref)
        inside = first >= 0
        low = jnp.where(inside, jnp.maximum(first, positions - WIN), 0)
        high = jnp.where(inside, jnp.minimum(last, positions + WIN), -1)
        low = as_column(low.astype(jnp.float32))
        high = as_column(high.astype(jnp.float32))
        for left in range(0, keys, LANES):
            key_at = (key_base + left + lax.broadcasted_iota(jnp.int32, (LANES, LANES), 1)).astype(jnp.float32)
            bias = jnp.where((key_at >= low) & (key_at <= high), jnp.float32(0.0), jnp.float32(NEG))
            store(top, count, left, bias[:count])


def head_pair(query, keys, values, bias):
    rows = query.shape[0]
    left = lax.broadcasted_iota(jnp.int32, query.shape, 1) < HSIZE
    nothing = jnp.zeros_like(query)
    both = jnp.concatenate([jnp.where(left, query, nothing), jnp.where(left, nothing, query)], axis=0)
    scores = lax.dot_general(both, keys, (((1,), (1,)), ((), ())), preferred_element_type=jnp.float32)
    scores = scores + jnp.concatenate([bias, bias], axis=0)
    row_max = jnp.max(scores, axis=1, keepdims=True)
    weights = jnp.exp2((scores - row_max) * EXP_SCALE).astype(jnp.bfloat16)
    mixed = jnp.dot(weights, values, preferred_element_type=jnp.float32)
    mixed = mixed[:, :LANES] / mixed[:, LANES:]
    keep = bias_any(bias)
    return jnp.where(keep, jnp.where(left, mixed[:rows], mixed[rows:]), 0.0).astype(jnp.bfloat16)


def bias_any(bias):
    return jnp.max(bias, axis=1, keepdims=True) > NEG / 2


def attend_inner(frames, starts_ref, lengths_ref, q_ref, k_ref, v_ref, o_ref, bias, wide):
    blocks = frames // WIN - 2
    anchor = lax.axis_index("seq") * frames

    @pl.when(pl.program_id(0) == 0)
    def _():
        wide[:, LANES:] = jnp.ones((frames, LANES), jnp.bfloat16)
        for i in range(blocks):
            def store(top, count, left, value):
                bias[i, top : top + count, left : left + LANES] = value

            band_bias(anchor + (i + 1) * WIN, WIN, anchor + i * WIN, 3 * WIN, starts_ref, lengths_ref, store)

    wide[:, :LANES] = v_ref[...]
    for i in range(blocks):
        window = slice(i * WIN, (i + 3) * WIN)
        o_ref[i * WIN : (i + 1) * WIN, :] = head_pair(
            q_ref[(i + 1) * WIN : (i + 2) * WIN, :], k_ref[window, :], wide[window, :], bias[i]
        )


def attend_ends(frames, starts_ref, lengths_ref, q_ref, k_ref, v_ref, before_ref, after_ref, o_ref, bias):
    anchor = lax.axis_index("seq") * frames
    own = SPAN - REACH

    @pl.when(pl.program_id(0) == 0)
    def _():
        for i, (base, key_base) in enumerate(((-EDGE, -REACH), (frames - WIN, frames - own))):
            def store(top, count, left, value):
                bias[i, top : top + count, left : left + LANES] = value

            band_bias(anchor + base, REACH, anchor + key_base, SPAN, starts_ref, lengths_ref, store)

    ones = jnp.ones((SPAN, LANES), jnp.bfloat16)
    for i in range(2):
        halo = (before_ref, after_ref)[i]
        mine = slice(0, own) if i == 0 else slice(frames - own, frames)

        def joined(far, near):
            return jnp.concatenate([far, near] if i == 0 else [near, far], axis=0)

        keys = joined(halo[:REACH, :], k_ref[mine, :])
        values = joined(halo[REACH : 2 * REACH, :], v_ref[mine, :])
        query = joined(halo[2 * REACH : 2 * REACH + EDGE, :], q_ref[:WIN, :] if i == 0 else q_ref[frames - WIN :, :])
        o_ref[i * REACH : (i + 1) * REACH, :] = head_pair(
            query, keys, jnp.concatenate([values, ones], axis=1), bias[i]
        )


def project(rows, own_ref, other_ref, w_own_ref, w_other_ref, res_ref, h_ref, stats_ref):
    width = h_ref.shape[1]
    step = 512
    total = jnp.zeros((rows, LANES), jnp.float32)
    for c in range(0, width, step):
        cols = slice(c, c + step)
        part = jnp.dot(own_ref[...], w_own_ref[:, cols], preferred_element_type=jnp.float32)
        part = part + jnp.dot(other_ref[...], w_other_ref[:, cols], preferred_element_type=jnp.float32)
        part = part + res_ref[:, cols].astype(jnp.float32)
        h_ref[:, cols] = part
        for l in range(0, step, LANES):
            total = total + part[:, l : l + LANES]
    mean = jnp.sum(total, axis=1, keepdims=True) * (1.0 / width)
    square = jnp.zeros((rows, LANES), jnp.float32)
    for c in range(0, width, LANES):
        off = h_ref[:, c : c + LANES] - mean
        square = square + off * off
    square = jnp.sum(square, axis=1, keepdims=True)
    for top in range(0, rows, LANES):
        count = min(LANES, rows - top)
        for k, column in enumerate((mean, square)):
            tile = jnp.broadcast_to(column[top : top + count], (count, LANES))
            if count < LANES:
                tile = jnp.concatenate([tile, jnp.zeros((LANES - count, LANES), jnp.float32)], axis=0)
            stats_ref[8 * k : 8 * k + 8, top : top + LANES] = jnp.transpose(tile)[:8, :]


def silu_add(hidden, conv_sum):
    half = conv_sum * 0.5
    return (hidden + (half + half * jnp.tanh(half))).astype(jnp.bfloat16)


def norm_conv(
    frames, starts_ref, lengths_ref, h_in_ref, h_end_ref, s_in_ref, t_in_ref, s_end_ref, t_end_ref, gain_ref, w_ref,
    o_ref, mean, scale, parity, normed, masked, flags,
):
    anchor = lax.axis_index("seq") * frames
    total = frames + 2 * EDGE
    chunk = 128
    width = 2.0 * h_in_ref.shape[1] * pl.num_programs(0)

    @pl.when(pl.program_id(0) == 0)
    def _():
        def place(at, count, base, own, other):
            positions = base + lax.broadcasted_iota(jnp.int32, (1, LANES), 1)
            index = jnp.zeros((1, LANES), jnp.int32) - 1
            for r in range(REC):
                start = starts_ref[r]
                inside = (positions >= start) & (positions < start + lengths_ref[r])
                index = jnp.where(inside, r, index)
            gap = own[0:1, :] - other[0:1, :]
            middle = 0.5 * (own[0:1, :] + other[0:1, :])
            var = (own[8:9, :] + other[8:9, :] + gap * gap * (width * 0.25)) * (1.0 / width)
            inverse = jnp.where(index >= 0, lax.rsqrt(var + 1e-5), 0.0)
            even = jnp.where(index >= 0, (index % 2).astype(jnp.float32), -1.0)
            mean[at : at + count, :] = as_column(middle)[:count]
            scale[at : at + count, :] = as_column(inverse)[:count]
            parity[at : at + count, :] = as_column(even)[:count]

        for top in range(0, frames - 2 * WIN, LANES):
            place(REACH + top, LANES, anchor + WIN + top, s_in_ref[:, top : top + LANES], t_in_ref[:, top : top + LANES])
        for i in range(2):
            for top, count in ((0, LANES), (LANES, EDGE)):
                lane = i * 2 * LANES + top

                def piece(ref):
                    return ref[:, lane : lane + LANES]

                base = (-EDGE if i == 0 else frames - WIN) + top
                ext = base + EDGE
                place(ext, count, anchor + base, piece(s_end_ref), piece(t_end_ref))
        for c in range(frames // chunk):
            count = jnp.int32(0)
            for r in range(REC):
                start = starts_ref[r] - anchor
                meets = (start < (c + 1) * chunk + KHALF) & (start + lengths_ref[r] > c * chunk - KHALF)
                count = count + meets.astype(jnp.int32)
            flags[c] = count

    gain = gain_ref[...]
    for source, at, count in (
        (h_end_ref[:REACH, :], 0, REACH),
        (h_in_ref[...], REACH, frames - 2 * WIN),
        (h_end_ref[REACH:, :], frames - WIN + EDGE, REACH),
    ):
        value = (source - mean[at : at + count, :]) * scale[at : at + count, :] * gain
        normed[at : at + count, :] = value.astype(jnp.bfloat16).astype(jnp.float32)

    def hidden_of(top, count):
        pieces = []
        for ref, at, lo, hi in (
            (h_end_ref, 0, -EDGE, WIN),
            (h_in_ref, 0, WIN, frames - WIN),
            (h_end_ref, REACH, frames - WIN, frames + EDGE),
        ):
            a, b = max(lo, top), min(hi, top + count)
            if a < b:
                pieces.append(ref[at + a - lo : at + b - lo, :])
        return pieces[0] if len(pieces) == 1 else jnp.concatenate(pieces, axis=0)

    def taps(load):
        acc = load(0) * w_ref[0:1, :]
        for tap in range(1, KERNEL):
            acc = acc + load(tap) * w_ref[tap : tap + 1, :]
        return acc

    for c in range(frames // chunk):
        top = c * chunk
        at = top + EDGE
        conv_sum = taps(lambda tap: normed[at - KHALF + tap : at - KHALF + tap + chunk, :])
        conv_sum = jnp.where(parity[at : at + chunk, :] >= 0, conv_sum, 0.0)
        o_ref[top : top + chunk, :] = silu_add(hidden_of(top, chunk), conv_sum)

    for c in range(frames // chunk):
        top = c * chunk
        at = top + EDGE

        @pl.when(flags[c] > 1)
        def _():
            conv_sum = jnp.zeros((chunk, LANES), jnp.float32)
            for side in range(2):
                masked[...] = jnp.where(
                    parity[at - EDGE : at + chunk + EDGE, :] == side, normed[at - EDGE : at + chunk + EDGE, :], 0.0
                )
                first = EDGE - KHALF
                part = taps(lambda tap: masked[first + tap : first + tap + chunk, :])
                conv_sum = jnp.where(parity[at : at + chunk, :] == side, part, conv_sum)
            o_ref[top : top + chunk, :] = silu_add(hidden_of(top, chunk), conv_sum)


def on_device(
    queries, attn_keys, attn_values, out_weight, residual, norm_gain, conv_weight, record_starts, record_lengths
):
    frames, heads_width = queries.shape
    width = residual.shape[1]
    pairs = heads_width // LANES
    inner = frames - 2 * WIN
    ends = 2 * REACH
    count = lax.axis_size("seq")
    swap = [(0, 1), (1, 0)]
    grid_params = pltpu.CompilerParams(vmem_limit_bytes=48 * 2**20)

    def payload(lo):
        def rows(array, n):
            return array[:n] if lo else array[-n:]

        edge = rows(residual, EDGE)
        return jnp.concatenate(
            [rows(attn_keys, REACH), rows(attn_values, REACH), rows(queries, EDGE), edge[:, :heads_width], edge[:, heads_width:]],
            axis=0,
        )

    after = lax.ppermute(payload(True), "seq", [(i + 1, i) for i in range(count - 1)])
    before = lax.ppermute(payload(False), "seq", [(i, i + 1) for i in range(count - 1)])
    weight_other = lax.ppermute(out_weight, "tp", swap)

    column = pl.BlockSpec((frames, LANES), lambda p: (0, p))
    attended_in = pl.pallas_call(
        functools.partial(attend_inner, frames),
        grid=(pairs,),
        out_shape=jax.ShapeDtypeStruct((inner, heads_width), jnp.bfloat16),
        in_specs=[SMEM, SMEM, column, column, column],
        out_specs=pl.BlockSpec((inner, LANES), lambda p: (0, p)),
        scratch_shapes=[
            pltpu.VMEM((inner // WIN, WIN, 3 * WIN), jnp.float32),
            pltpu.VMEM((frames, 2 * LANES), jnp.bfloat16),
        ],
        compiler_params=grid_params,
        name="attend_inner",
    )(record_starts, record_lengths, queries, attn_keys, attn_values)

    halo = pl.BlockSpec((before.shape[0], LANES), lambda p: (0, p))
    attended_end = pl.pallas_call(
        functools.partial(attend_ends, frames),
        grid=(pairs,),
        out_shape=jax.ShapeDtypeStruct((ends, heads_width), jnp.bfloat16),
        in_specs=[SMEM, SMEM, column, column, column, halo, halo],
        out_specs=pl.BlockSpec((ends, LANES), lambda p: (0, p)),
        scratch_shapes=[pltpu.VMEM((2, REACH, SPAN), jnp.float32)],
        compiler_params=grid_params,
        name="attend_ends",
    )(record_starts, record_lengths, queries, attn_keys, attn_values, before, after)

    mine = lax.axis_index("tp").astype(jnp.int32).reshape(1)

    def projection(own, other, res, tile, name):
        rows = own.shape[0]
        padded = -(-tile // LANES) * LANES
        return pl.pallas_call(
            lambda t_ref, *refs: project(tile, *refs),
            grid_spec=pltpu.PrefetchScalarGridSpec(
                num_scalar_prefetch=1,
                grid=(rows // tile,),
                in_specs=[
                    pl.BlockSpec((tile, heads_width), lambda i, t: (i, 0)),
                    pl.BlockSpec((tile, heads_width), lambda i, t: (i, 0)),
                    pl.BlockSpec((heads_width, width), lambda i, t: (0, t[0])),
                    pl.BlockSpec((heads_width, width), lambda i, t: (0, t[0])),
                    pl.BlockSpec((tile, width), lambda i, t: (i, 0)),
                ],
                out_specs=[
                    pl.BlockSpec((tile, width), lambda i, t: (i, 0)),
                    pl.BlockSpec((16, padded), lambda i, t: (0, i)),
                ],
            ),
            out_shape=[
                jax.ShapeDtypeStruct((rows, width), jnp.float32),
                jax.ShapeDtypeStruct((16, rows // tile * padded), jnp.float32),
            ],
            compiler_params=grid_params,
            name=name,
        )(mine, own, other, out_weight, weight_other, res)

    other_in = lax.ppermute(attended_in, "tp", swap)
    hidden_in, stats_in = projection(attended_in, other_in, residual[WIN : frames - WIN], 128, "project_inner")
    other_stats_in = lax.ppermute(stats_in, "tp", swap)

    def edge_rows(received):
        tail = received[2 * REACH + EDGE :]
        return jnp.concatenate([tail[:EDGE], tail[EDGE:]], axis=1)

    residual_end = jnp.concatenate(
        [edge_rows(before), residual[:WIN], residual[frames - WIN :], edge_rows(after)], axis=0
    )
    other_end = lax.ppermute(attended_end, "tp", swap)
    hidden_end, stats_end = projection(attended_end, other_end, residual_end, REACH, "project_ends")
    other_stats_end = lax.ppermute(stats_end, "tp", swap)

    total = frames + 2 * EDGE
    whole = lambda array: pl.BlockSpec(array.shape, lambda g: (0, 0))
    lane_block = lambda n: pl.BlockSpec((n, LANES), lambda g: (0, g))
    return pl.pallas_call(
        functools.partial(norm_conv, frames),
        grid=(width // LANES,),
        out_shape=jax.ShapeDtypeStruct((frames, width), jnp.bfloat16),
        in_specs=[
            SMEM, SMEM, lane_block(inner), lane_block(ends),
            whole(stats_in), whole(stats_in), whole(stats_end), whole(stats_end),
            lane_block(1), lane_block(KERNEL),
        ],
        out_specs=lane_block(frames),
        scratch_shapes=[
            pltpu.VMEM((total, LANES), jnp.float32),
            pltpu.VMEM((total, LANES), jnp.float32),
            pltpu.VMEM((total, LANES), jnp.float32),
            pltpu.VMEM((total, LANES), jnp.float32),
            pltpu.VMEM((128 + 2 * EDGE, LANES), jnp.float32),
            pltpu.SMEM((frames // 128,), jnp.int32),
        ],
        compiler_params=grid_params,
        name="norm_conv",
    )(
        record_starts, record_lengths, hidden_in, hidden_end, stats_in, other_stats_in, stats_end, other_stats_end,
        norm_gain.reshape(1, width), conv_weight,
    )


def solution(mesh):
    placed = (
        P(("grp", "seq"), "tp"),
        P(("grp", "seq"), "tp"),
        P(("grp", "seq"), "tp"),
        P("tp", None),
        P(("grp", "seq"), "tp"),
        P("tp"),
        P(None, "tp"),
        P("grp"),
        P("grp"),
    )
    return jax.shard_map(
        on_device, mesh=mesh, in_specs=placed, out_specs=P(("grp", "seq"), "tp"), check_vma=False
    )
```

```python
import functools

import jax
import jax.numpy as jnp
from jax import lax
from jax.experimental import pallas as pl
from jax.experimental.pallas import tpu as pltpu
from jax.sharding import PartitionSpec as P

D = 3072
HSIZE = 64
WIN = 128
KHALF = 15
REC = 8
KERNEL = 31
EDGE = 16
REACH = WIN + EDGE
SPAN = 512
LANES = 128
NEG = -1e30
EXP_SCALE = HSIZE ** (-0.5) * 1.4426950408889634
SMEM = pl.BlockSpec(memory_space=pltpu.SMEM)


def row_bounds(positions, starts_ref, lengths_ref):
    first = jnp.full(positions.shape, -1, jnp.int32)
    last = jnp.full(positions.shape, -2, jnp.int32)
    for r in range(REC):
        start = starts_ref[r]
        end = start + lengths_ref[r]
        inside = (positions >= start) & (positions < end)
        first = jnp.where(inside, start, first)
        last = jnp.where(inside, end - 1, last)
    return first, last


def as_column(row):
    return jnp.transpose(jnp.broadcast_to(row, (LANES, LANES)))


def band_bias(base, rows, key_base, keys, starts_ref, lengths_ref, store):
    for top in range(0, rows, LANES):
        count = min(LANES, rows - top)
        positions = base + top + lax.broadcasted_iota(jnp.int32, (1, LANES), 1)
        first, last = row_bounds(positions, starts_ref, lengths_ref)
        inside = first >= 0
        low = jnp.where(inside, jnp.maximum(first, positions - WIN), 0)
        high = jnp.where(inside, jnp.minimum(last, positions + WIN), -1)
        low = as_column(low.astype(jnp.float32))
        high = as_column(high.astype(jnp.float32))
        for left in range(0, keys, LANES):
            key_at = (key_base + left + lax.broadcasted_iota(jnp.int32, (LANES, LANES), 1)).astype(jnp.float32)
            bias = jnp.where((key_at >= low) & (key_at <= high), jnp.float32(0.0), jnp.float32(NEG))
            store(top, count, left, bias[:count])


def head_pair(query, keys, values, bias):
    rows = query.shape[0]
    left = lax.broadcasted_iota(jnp.int32, query.shape, 1) < HSIZE
    nothing = jnp.zeros_like(query)
    both = jnp.concatenate([jnp.where(left, query, nothing), jnp.where(left, nothing, query)], axis=0)
    scores = lax.dot_general(both, keys, (((1,), (1,)), ((), ())), preferred_element_type=jnp.float32)
    scores = scores + jnp.concatenate([bias, bias], axis=0)
    row_max = jnp.max(scores, axis=1, keepdims=True)
    weights = jnp.exp2((scores - row_max) * EXP_SCALE).astype(jnp.bfloat16)
    mixed = jnp.dot(weights, values, preferred_element_type=jnp.float32)
    mixed = mixed[:, :LANES] / mixed[:, LANES:]
    keep = bias_any(bias)
    return jnp.where(keep, jnp.where(left, mixed[:rows], mixed[rows:]), 0.0).astype(jnp.bfloat16)


def bias_any(bias):
    return jnp.max(bias, axis=1, keepdims=True) > NEG / 2


def attend_inner(frames, starts_ref, lengths_ref, q_ref, k_ref, v_ref, o_ref, bias, wide):
    blocks = frames // WIN - 2
    anchor = lax.axis_index("seq") * frames

    @pl.when(pl.program_id(0) == 0)
    def _():
        wide[:, LANES:] = jnp.ones((frames, LANES), jnp.bfloat16)
        for i in range(blocks):
            def store(top, count, left, value):
                bias[i, top : top + count, left : left + LANES] = value

            band_bias(anchor + (i + 1) * WIN, WIN, anchor + i * WIN, 3 * WIN, starts_ref, lengths_ref, store)

    wide[:, :LANES] = v_ref[...]
    for i in range(blocks):
        window = slice(i * WIN, (i + 3) * WIN)
        o_ref[i * WIN : (i + 1) * WIN, :] = head_pair(
            q_ref[(i + 1) * WIN : (i + 2) * WIN, :], k_ref[window, :], wide[window, :], bias[i]
        )


def attend_ends(frames, starts_ref, lengths_ref, q_ref, k_ref, v_ref, before_ref, after_ref, o_ref, bias):
    anchor = lax.axis_index("seq") * frames
    own = SPAN - REACH

    @pl.when(pl.program_id(0) == 0)
    def _():
        for i, (base, key_base) in enumerate(((-EDGE, -REACH), (frames - WIN, frames - own))):
            def store(top, count, left, value):
                bias[i, top : top + count, left : left + LANES] = value

            band_bias(anchor + base, REACH, anchor + key_base, SPAN, starts_ref, lengths_ref, store)

    ones = jnp.ones((SPAN, LANES), jnp.bfloat16)
    for i in range(2):
        halo = (before_ref, after_ref)[i]
        mine = slice(0, own) if i == 0 else slice(frames - own, frames)

        def joined(far, near):
            return jnp.concatenate([far, near] if i == 0 else [near, far], axis=0)

        keys = joined(halo[3 * EDGE : 3 * EDGE + REACH, :], k_ref[mine, :])
        values = joined(halo[3 * EDGE + REACH :, :], v_ref[mine, :])
        query = joined(halo[2 * EDGE : 3 * EDGE, :], q_ref[:WIN, :] if i == 0 else q_ref[frames - WIN :, :])
        o_ref[i * REACH : (i + 1) * REACH, :] = head_pair(
            query, keys, jnp.concatenate([values, ones], axis=1), bias[i]
        )


def pack_edges(frames, q_ref, k_ref, v_ref, r_ref, top_ref, bottom_ref, sems):
    half = q_ref.shape[1]
    copies = []
    for i, out in enumerate((top_ref, bottom_ref)):
        def rows(ref, n):
            return ref.at[pl.ds(0 if i == 0 else frames - n, n), :]

        moves = [
            (r_ref.at[pl.ds(0 if i == 0 else frames - EDGE, EDGE), pl.ds(0, half)], 0, EDGE),
            (r_ref.at[pl.ds(0 if i == 0 else frames - EDGE, EDGE), pl.ds(half, half)], EDGE, EDGE),
            (rows(q_ref, EDGE), 2 * EDGE, EDGE),
            (rows(k_ref, REACH), 3 * EDGE, REACH),
            (rows(v_ref, REACH), 3 * EDGE + REACH, REACH),
        ]
        for n, (source, at, count) in enumerate(moves):
            copies.append(pltpu.make_async_copy(source, out.at[pl.ds(at, count), :], sems.at[i, n]))
    for copy in copies:
        copy.start()
    for copy in copies:
        copy.wait()


def project(own_ref, other_ref, w_own_ref, w_other_ref, residual, h_ref, stats_ref, shift, first, second, tiles, total_width):
    step = pl.program_id(tiles[0])
    rows, width = h_ref.shape
    part = jnp.dot(own_ref[...], w_own_ref[...], preferred_element_type=jnp.float32)
    part = part + jnp.dot(other_ref[...], w_other_ref[...], preferred_element_type=jnp.float32)
    part = part + residual
    h_ref[...] = part

    @pl.when(step == 0)
    def _():
        mean = jnp.sum(part, axis=1, keepdims=True) * (1.0 / width)
        shift[...] = jnp.broadcast_to(mean, (rows, LANES))
        first[...] = jnp.zeros_like(first)
        second[...] = jnp.zeros_like(second)

    one, two = first[...], second[...]
    for l in range(0, width, LANES):
        off = part[:, l : l + LANES] - shift[...]
        one = one + off
        two = two + off * off
    first[...] = one
    second[...] = two

    @pl.when(step == tiles[1] - 1)
    def _():
        moved = jnp.sum(first[...], axis=1, keepdims=True) * (1.0 / total_width)
        mean = shift[...] + moved
        square = jnp.sum(second[...], axis=1, keepdims=True) - moved * moved * total_width
        for top in range(0, rows, LANES):
            count = min(LANES, rows - top)
            for k, column in enumerate((mean, jnp.broadcast_to(square, (rows, LANES)))):
                tile = column[top : top + count]
                if count < LANES:
                    tile = jnp.concatenate([tile, jnp.zeros((LANES - count, LANES), jnp.float32)], axis=0)
                stats_ref[8 * k : 8 * k + 8, top : top + LANES] = jnp.transpose(tile)[:8, :]


def project_inner(tiles, t_ref, own, other, w_own, w_other, res, h_ref, stats, shift, first, second):
    top = WIN
    project(
        own, other, w_own, w_other, res[top : top + h_ref.shape[0], :].astype(jnp.float32),
        h_ref, stats, shift, first, second, (0, tiles), float(tiles * h_ref.shape[1]),
    )


def project_ends(tiles, t_ref, own, other, w_own, w_other, res, before, after, h_ref, stats, shift, first, second):
    frames = res.shape[0]
    residual = jnp.concatenate([before[...], res[:WIN, :], res[frames - WIN :, :], after[...]], axis=0)
    project(
        own, other, w_own, w_other, residual.astype(jnp.float32),
        h_ref, stats, shift, first, second, (0, tiles), float(tiles * h_ref.shape[1]),
    )


def stat_columns(base, own, other, width, starts_ref, lengths_ref):
    positions = base + lax.broadcasted_iota(jnp.int32, (1, LANES), 1)
    index = jnp.zeros((1, LANES), jnp.int32) - 1
    for r in range(REC):
        start = starts_ref[r]
        inside = (positions >= start) & (positions < start + lengths_ref[r])
        index = jnp.where(inside, r, index)
    gap = own[0:1, :] - other[0:1, :]
    middle = 0.5 * (own[0:1, :] + other[0:1, :])
    var = (own[8:9, :] + other[8:9, :] + gap * gap * (width * 0.25)) * (1.0 / width)
    inverse = jnp.where(index >= 0, lax.rsqrt(var + 1e-5), 0.0)
    parity = jnp.where(index >= 0, (index % 2).astype(jnp.float32), -1.0)
    return as_column(middle), as_column(inverse), as_column(parity)


def mark_mixed(base, chunks, flags, at, starts_ref, lengths_ref):
    flags[at] = jnp.int32(0)
    for r in range(REC - 1):
        end, start = starts_ref[r] + lengths_ref[r], starts_ref[r + 1]
        low = jnp.maximum((end - KHALF - base) >> 4, 0)
        high = jnp.minimum((start + KHALF - base + EDGE - 1) >> 4, chunks)

        @pl.when(start - end < KHALF)
        def _():
            def add(c, carry):
                known = flags[at]
                flags[at + 1 + known] = c
                flags[at] = known + 1
                return carry

            lax.fori_loop(low, high, add, 0)


def convolve(load, w_ref):
    acc = load(0) * w_ref[0:1, :]
    for tap in range(1, KERNEL):
        acc = acc + load(tap) * w_ref[tap : tap + 1, :]
    return acc


def differences(x_ref, diffs):
    rows = x_ref.shape[0]
    x = x_ref[...]
    near = x[: rows - 8] - x[8:]
    diffs[0, : rows - 8, :] = near
    diffs[1, : rows - 16, :] = x[: rows - 16] - x[16:]
    diffs[2, : rows - 24, :] = near[: rows - 24] - near[16:]


def tap_sums(w_ref, wq):
    padded = jnp.concatenate([jnp.zeros((1, LANES), jnp.float32), w_ref[...]], axis=0)
    w0, w1, w2, w3 = (padded[8 * j : 8 * j + 8] for j in range(4))
    for n, value in enumerate((w0, w0 + w1, -w1, w0 + w2, w0 + w1 + w2 + w3, -(w1 + w3), -w2, -(w2 + w3), w3)):
        wq[n] = value


def conv_group(x_ref, diffs, wq, at):
    sources = (
        (diffs.at[2], 0), (diffs.at[1], 8), (diffs.at[2], 8),
        (diffs.at[0], 16), (x_ref, 24), (diffs.at[0], 24),
        (diffs.at[2], 16), (diffs.at[1], 24), (diffs.at[2], 24),
    )
    sums = [None] * 9
    for s in range(8):
        for n, (ref, off) in enumerate(sources):
            first = at - EDGE + s + off
            term = ref[first : first + 8, :] * wq[n, s : s + 1, :]
            sums[n] = term if sums[n] is None else sums[n] + term
    a0, a1 = sums[1] + sums[0], sums[1] + sums[2]
    p0, p1 = sums[4] + sums[3], sums[4] + sums[5]
    c0, c1 = sums[7] + sums[6], sums[7] + sums[8]
    return jnp.concatenate([a0 + p0, a1 + p1, p0 + c0, p1 + c1], axis=0)


def silu_add(hidden, conv_sum):
    half = conv_sum * 0.5
    return (hidden + (half + half * jnp.tanh(half))).astype(jnp.bfloat16)


def conv_rows(rows, hidden, normed, parity, diffs, wq, masked, flags, flag_at, w_ref, out):
    differences(normed, diffs)
    group = 2 * EDGE
    for top in list(range(0, rows - group, group)) + [rows - group]:
        at = top + EDGE
        conv_sum = conv_group(normed, diffs, wq, at)
        conv_sum = jnp.where(parity[at : at + group, :] >= 0, conv_sum, 0.0)
        out[top : top + group, :] = silu_add(hidden[at : at + group, :], conv_sum)

    def again(c, carry):
        top = pl.multiple_of(flags[flag_at + 1 + c] * EDGE, EDGE)
        around, here = pl.ds(top, 3 * EDGE), pl.ds(top + EDGE, EDGE)
        conv_sum = jnp.zeros((EDGE, LANES), jnp.float32)
        for side in range(2):
            masked[...] = jnp.where(parity[around, :] == side, normed[around, :], 0.0)
            first = EDGE - KHALF
            part = convolve(lambda tap: masked[first + tap : first + tap + EDGE, :], w_ref)
            conv_sum = jnp.where(parity[here, :] == side, part, conv_sum)
        out[pl.ds(top, EDGE), :] = silu_add(hidden[here, :], conv_sum)
        return carry

    lax.fori_loop(0, flags[flag_at], again, 0)


def norm_conv_inner(
    frames, starts_ref, lengths_ref, h_ref, own_ref, other_ref, gain_ref, w_ref, o_ref,
    mean, scale, parity, normed, diffs, wq, masked, out, flags, sems,
):
    step, steps = pl.program_id(0), pl.num_programs(0)
    rows = frames - 2 * WIN
    kept = rows - 2 * EDGE
    base = lax.axis_index("seq") * frames + WIN

    @pl.when(step == 0)
    def _():
        width = 2.0 * LANES * steps
        for top in range(0, rows, LANES):
            here = slice(top, top + LANES)
            mean[here, :], scale[here, :], parity[here, :] = stat_columns(
                base + top, own_ref[:, here], other_ref[:, here], width, starts_ref, lengths_ref
            )
        mark_mixed(base + EDGE, kept // EDGE, flags, 0, starts_ref, lengths_ref)

    value = (h_ref[...] - mean[...]) * scale[...] * gain_ref[...]
    normed[...] = value.astype(jnp.bfloat16).astype(jnp.float32)
    slot = step % 2

    def copy(at, which):
        return pltpu.make_async_copy(
            out.at[which], o_ref.at[pl.ds(WIN + EDGE, kept), pl.ds(pl.multiple_of(at * LANES, LANES), LANES)], sems.at[which]
        )

    @pl.when(step >= 2)
    def _():
        copy(step - 2, slot).wait()

    tap_sums(w_ref, wq)
    conv_rows(kept, h_ref, normed, parity, diffs, wq, masked, flags, 0, w_ref, out.at[slot])
    copy(step, slot).start()

    @pl.when(step == steps - 1)
    def _():
        copy(step - 1, 1 - slot).wait()
        copy(step, slot).wait()


def norm_conv_ends(
    frames, starts_ref, lengths_ref, h_end_ref, h_low_ref, h_high_ref, s_end_ref, t_end_ref, s_in_ref, t_in_ref,
    gain_ref, w_ref, done_ref, o_ref, mean, scale, parity, hidden, normed, diffs, wq, masked, out, flags, sems,
):
    step, steps = pl.program_id(0), pl.num_programs(0)
    inner = frames - 2 * WIN
    anchor = lax.axis_index("seq") * frames
    more = 2 * EDGE
    rows = REACH + more

    @pl.when(step == 0)
    def _():
        width = 2.0 * LANES * steps

        def place(i, at, count, base, lane, own, other, skip):
            values = stat_columns(
                base, own[:, lane : lane + LANES], other[:, lane : lane + LANES], width, starts_ref, lengths_ref
            )
            for ref, value in zip((mean, scale, parity), values):
                ref[i, at : at + count, :] = value[skip : skip + count]

        for top, count in ((0, LANES), (LANES, EDGE)):
            place(0, top, count, anchor - EDGE + top, top, s_end_ref, t_end_ref, 0)
        place(0, REACH, more, anchor + WIN, 0, s_in_ref, t_in_ref, 0)
        place(1, 0, more, anchor + frames - 2 * WIN, inner - LANES, s_in_ref, t_in_ref, LANES - more)
        own = jnp.concatenate([s_end_ref[:, LANES : 2 * LANES], s_end_ref[:, 2 * LANES :]], axis=1)[:, EDGE : EDGE + 2 * LANES - EDGE]
        other = jnp.concatenate([t_end_ref[:, LANES : 2 * LANES], t_end_ref[:, 2 * LANES :]], axis=1)[:, EDGE : EDGE + 2 * LANES - EDGE]
        place(1, more, LANES, anchor + frames - WIN, 0, own, other, 0)
        tail = jnp.concatenate([s_end_ref[:, 2 * LANES + EDGE :], jnp.zeros((16, LANES), jnp.float32)], axis=1)
        tail2 = jnp.concatenate([t_end_ref[:, 2 * LANES + EDGE :], jnp.zeros((16, LANES), jnp.float32)], axis=1)
        place(1, more + LANES, EDGE, anchor + frames, 0, tail, tail2, 0)
        for i in range(2):
            mark_mixed(anchor + i * (frames - REACH), REACH // EDGE, flags, i * 64, starts_ref, lengths_ref)

    hidden[0, :REACH, :] = h_end_ref[:REACH, :]
    hidden[0, REACH:, :] = h_low_ref[...]
    hidden[1, :more, :] = h_high_ref[...]
    hidden[1, more:, :] = h_end_ref[REACH:, :]
    slot = step % 2

    def copies(at, which):
        lanes = pl.ds(pl.multiple_of(at * LANES, LANES), LANES)
        return [
            pltpu.make_async_copy(
                out.at[which, i], o_ref.at[pl.ds(i * (frames - REACH), REACH), lanes], sems.at[which, i]
            )
            for i in range(2)
        ]

    @pl.when(step >= 2)
    def _():
        for copy in copies(step - 2, slot):
            copy.wait()

    tap_sums(w_ref, wq)
    for i in range(2):
        value = (hidden[i] - mean[i]) * scale[i] * gain_ref[...]
        normed[i] = value.astype(jnp.bfloat16).astype(jnp.float32)
        conv_rows(
            REACH, hidden.at[i], normed.at[i], parity.at[i], diffs.at[i], wq, masked, flags, i * 64, w_ref, out.at[slot, i]
        )
    for copy in copies(step, slot):
        copy.start()

    @pl.when(step == steps - 1)
    def _():
        for copy in copies(step - 1, 1 - slot) + copies(step, slot):
            copy.wait()


def cost(microseconds):
    return pl.CostEstimate(flops=int(microseconds * 4e8), bytes_accessed=1000, transcendentals=0)


def params(mebibytes):
    return pltpu.CompilerParams(vmem_limit_bytes=mebibytes * 2**20)


def on_device(
    queries, attn_keys, attn_values, out_weight, residual, norm_gain, conv_weight, record_starts, record_lengths
):
    frames, heads_width = queries.shape
    width = residual.shape[1]
    pairs = heads_width // LANES
    inner = frames - 2 * WIN
    ends = 2 * REACH
    count = lax.axis_size("seq")
    swap = [(0, 1), (1, 0)]
    anywhere = pl.BlockSpec(memory_space=pl.ANY)

    edges = jax.ShapeDtypeStruct((3 * EDGE + 2 * REACH, heads_width), jnp.bfloat16)
    top_edge, bottom_edge = pl.pallas_call(
        functools.partial(pack_edges, frames),
        out_shape=[edges, edges],
        in_specs=[pl.BlockSpec(memory_space=pltpu.HBM)] * 4,
        out_specs=[pl.BlockSpec(memory_space=pltpu.VMEM)] * 2,
        scratch_shapes=[pltpu.SemaphoreType.DMA((2, 5))],
        compiler_params=params(60),
        name="pack_edges",
    )(queries, attn_keys, attn_values, residual)
    top_edge, bottom_edge, queries = lax.optimization_barrier((top_edge, bottom_edge, queries))
    after = lax.ppermute(top_edge, "seq", [(i + 1, i) for i in range(count - 1)])
    before = lax.ppermute(bottom_edge, "seq", [(i, i + 1) for i in range(count - 1)])
    weight_other = lax.ppermute(out_weight, "tp", swap)

    column = pl.BlockSpec((frames, LANES), lambda p: (0, p))
    attended_in = pl.pallas_call(
        functools.partial(attend_inner, frames),
        grid=(pairs,),
        out_shape=jax.ShapeDtypeStruct((inner, heads_width), jnp.bfloat16),
        in_specs=[SMEM, SMEM, column, column, column],
        out_specs=pl.BlockSpec((inner, LANES), lambda p: (0, p)),
        scratch_shapes=[
            pltpu.VMEM((inner // WIN, WIN, 3 * WIN), jnp.float32),
            pltpu.VMEM((frames, 2 * LANES), jnp.bfloat16),
        ],
        compiler_params=params(16),
        cost_estimate=cost(0.2),
        name="attend_inner",
    )(record_starts, record_lengths, queries, attn_keys, attn_values)

    mine = lax.axis_index("tp").astype(jnp.int32).reshape(1)
    step = 256
    tiles = width // step

    def projection(body, own, other, extra, extra_specs, microseconds, name):
        rows = own.shape[0]
        padded = -(-rows // LANES) * LANES
        return pl.pallas_call(
            functools.partial(body, tiles),
            grid_spec=pltpu.PrefetchScalarGridSpec(
                num_scalar_prefetch=1,
                grid=(tiles,),
                in_specs=[
                    pl.BlockSpec((rows, heads_width), lambda j, t: (0, 0)),
                    pl.BlockSpec((rows, heads_width), lambda j, t: (0, 0)),
                    pl.BlockSpec((heads_width, step), lambda j, t: (0, t[0] * tiles + j)),
                    pl.BlockSpec((heads_width, step), lambda j, t: (0, t[0] * tiles + j)),
                    pl.BlockSpec((frames, step), lambda j, t: (0, j)),
                ]
                + extra_specs,
                out_specs=[
                    pl.BlockSpec((rows, step), lambda j, t: (0, j)),
                    pl.BlockSpec((16, padded), lambda j, t: (0, 0)),
                ],
                scratch_shapes=[pltpu.VMEM((rows, LANES), jnp.float32)] * 3,
            ),
            out_shape=[
                jax.ShapeDtypeStruct((rows, width), jnp.float32),
                jax.ShapeDtypeStruct((16, padded), jnp.float32),
            ],
            compiler_params=params(20),
            cost_estimate=cost(microseconds),
            name=name,
        )(mine, own, other, out_weight, weight_other, residual, *extra)

    other_in = lax.ppermute(attended_in, "tp", swap)
    hidden_in, stats_in = projection(project_inner, attended_in, other_in, [], [], 0.2, "project_inner")
    other_stats_in = lax.ppermute(stats_in, "tp", swap)

    whole = lambda array: pl.BlockSpec(array.shape, lambda g: (0, 0))
    lane_block = lambda n, i=0: pl.BlockSpec((n, LANES), lambda g: (i, g))
    gain = norm_gain.reshape(1, width)
    shared = lambda n: pltpu.VMEM(n + (LANES,), jnp.float32)
    kept = inner - 2 * EDGE
    result = jax.ShapeDtypeStruct((frames, width), jnp.bfloat16)
    partly = pl.pallas_call(
        functools.partial(norm_conv_inner, frames),
        grid=(width // LANES,),
        out_shape=result,
        in_specs=[SMEM, SMEM, lane_block(inner), whole(stats_in), whole(stats_in), lane_block(1), lane_block(KERNEL)],
        out_specs=anywhere,
        scratch_shapes=[
            shared((inner,)), shared((inner,)), shared((inner,)), shared((inner,)), shared((3, inner)), shared((9, 8)),
            shared((3 * EDGE,)),
            pltpu.VMEM((2, kept, LANES), jnp.bfloat16),
            pltpu.SMEM((64,), jnp.int32),
            pltpu.SemaphoreType.DMA((2,)),
        ],
        compiler_params=params(16),
        cost_estimate=cost(0.2),
        name="norm_conv_inner",
    )(record_starts, record_lengths, hidden_in, stats_in, other_stats_in, gain, conv_weight)

    before, after, partly = lax.optimization_barrier((before, after, partly))
    halo = pl.BlockSpec((before.shape[0], LANES), lambda p: (0, p))
    attended_end = pl.pallas_call(
        functools.partial(attend_ends, frames),
        grid=(pairs,),
        out_shape=jax.ShapeDtypeStruct((ends, heads_width), jnp.bfloat16),
        in_specs=[SMEM, SMEM, column, column, column, halo, halo],
        out_specs=pl.BlockSpec((ends, LANES), lambda p: (0, p)),
        scratch_shapes=[pltpu.VMEM((2, REACH, SPAN), jnp.float32)],
        compiler_params=params(16),
        cost_estimate=cost(5),
        name="attend_ends",
    )(record_starts, record_lengths, queries, attn_keys, attn_values, before, after)

    def edge_rows(received):
        return jnp.concatenate([received[:EDGE], received[EDGE : 2 * EDGE]], axis=1)

    other_end = lax.ppermute(attended_end, "tp", swap)
    sliver = pl.BlockSpec((EDGE, step), lambda j, t: (0, j))
    hidden_end, stats_end = projection(
        project_ends, attended_end, other_end, [edge_rows(before), edge_rows(after)], [sliver, sliver], 4, "project_ends"
    )
    other_stats_end = lax.ppermute(stats_end, "tp", swap)

    more = 2 * EDGE
    rows = REACH + more
    return pl.pallas_call(
        functools.partial(norm_conv_ends, frames),
        grid=(width // LANES,),
        out_shape=result,
        in_specs=[
            SMEM, SMEM, lane_block(ends), lane_block(more), lane_block(more, inner // more - 1),
            whole(stats_end), whole(stats_end), whole(stats_in), whole(stats_in), lane_block(1), lane_block(KERNEL),
            anywhere,
        ],
        out_specs=anywhere,
        scratch_shapes=[
            shared((2, rows)), shared((2, rows)), shared((2, rows)), shared((2, rows)), shared((2, rows)),
            shared((2, 3, rows)), shared((9, 8)), shared((3 * EDGE,)),
            pltpu.VMEM((2, 2, REACH, LANES), jnp.bfloat16),
            pltpu.SMEM((128,), jnp.int32),
            pltpu.SemaphoreType.DMA((2, 2)),
        ],
        input_output_aliases={11: 0},
        compiler_params=params(16),
        cost_estimate=cost(5),
        name="norm_conv_ends",
    )(
        record_starts, record_lengths, hidden_end, hidden_in, hidden_in, stats_end, other_stats_end, stats_in,
        other_stats_in, gain, conv_weight, partly,
    )


def solution(mesh):
    placed = (
        P(("grp", "seq"), "tp"),
        P(("grp", "seq"), "tp"),
        P(("grp", "seq"), "tp"),
        P("tp", None),
        P(("grp", "seq"), "tp"),
        P("tp"),
        P(None, "tp"),
        P("grp"),
        P("grp"),
    )
    return jax.shard_map(
        on_device, mesh=mesh, in_specs=placed, out_specs=P(("grp", "seq"), "tp"), check_vma=False
    )
```

```python
import functools

import jax
import jax.numpy as jnp
from jax import lax
from jax.experimental import pallas as pl
from jax.experimental.pallas import tpu as pltpu
from jax.sharding import PartitionSpec as P

D = 3072
HSIZE = 64
WIN = 128
KHALF = 15
REC = 8
KERNEL = 31
EDGE = 16
REACH = WIN + EDGE
SPAN = 512
LANES = 128
NEG = -1e30
SHARE = 4
EXP_SCALE = HSIZE ** (-0.5) * 1.4426950408889634
SMEM = pl.BlockSpec(memory_space=pltpu.SMEM)


def row_bounds(positions, starts_ref, lengths_ref):
    first = jnp.full(positions.shape, -1, jnp.int32)
    last = jnp.full(positions.shape, -2, jnp.int32)
    for r in range(REC):
        start = starts_ref[r]
        end = start + lengths_ref[r]
        inside = (positions >= start) & (positions < end)
        first = jnp.where(inside, start, first)
        last = jnp.where(inside, end - 1, last)
    return first, last


def as_column(row):
    return jnp.transpose(jnp.broadcast_to(row, (LANES, LANES)))


def band_bias(base, rows, key_base, keys, starts_ref, lengths_ref, store):
    for top in range(0, rows, LANES):
        count = min(LANES, rows - top)
        positions = base + top + lax.broadcasted_iota(jnp.int32, (1, LANES), 1)
        first, last = row_bounds(positions, starts_ref, lengths_ref)
        inside = first >= 0
        low = jnp.where(inside, jnp.maximum(first, positions - WIN), 0)
        high = jnp.where(inside, jnp.minimum(last, positions + WIN), -1)
        low = as_column(low.astype(jnp.float32))
        high = as_column(high.astype(jnp.float32))
        for left in range(0, keys, LANES):
            key_at = (key_base + left + lax.broadcasted_iota(jnp.int32, (LANES, LANES), 1)).astype(jnp.float32)
            bias = jnp.where((key_at >= low) & (key_at <= high), jnp.float32(0.0), jnp.float32(NEG))
            store(top, count, left, bias[:count])


def head_pair(query, keys, values, bias):
    rows = query.shape[0]
    left = lax.broadcasted_iota(jnp.int32, query.shape, 1) < HSIZE
    nothing = jnp.zeros_like(query)
    both = jnp.concatenate([jnp.where(left, query, nothing), jnp.where(left, nothing, query)], axis=0)
    scores = lax.dot_general(both, keys, (((1,), (1,)), ((), ())), preferred_element_type=jnp.float32)
    scores = scores + jnp.concatenate([bias, bias], axis=0)
    row_max = jnp.max(scores, axis=1, keepdims=True)
    weights = jnp.exp2((scores - row_max) * EXP_SCALE).astype(jnp.bfloat16)
    mixed = jnp.dot(weights, values, preferred_element_type=jnp.float32)
    mixed = mixed[:, :LANES] / mixed[:, LANES:]
    keep = bias_any(bias)
    return jnp.where(keep, jnp.where(left, mixed[:rows], mixed[rows:]), 0.0).astype(jnp.bfloat16)


def bias_any(bias):
    return jnp.max(bias, axis=1, keepdims=True) > NEG / 2


def split_heads(array):
    left = lax.broadcasted_iota(jnp.int32, array.shape, 1) < HSIZE
    nothing = jnp.zeros_like(array)
    return jnp.where(left, array, nothing), jnp.where(left, nothing, array)


def start_all(copies):
    for copy in copies:
        copy.start()
    return copies


def wait_all(copies):
    for copy in copies:
        copy.wait()


def attend_inner(
    frames, starts_ref, lengths_ref, q_hbm, k_hbm, v_hbm, w_hbm, r_hbm, o_ref, w_own_ref, r_in_ref,
    columns, bias, keys, values, sems, more_sems
):
    blocks = frames // WIN - 2
    span = 3 * WIN
    pairs = q_hbm.shape[1] // LANES
    anchor = lax.axis_index("seq") * frames

    def fetch(p):
        lanes = pl.ds(p * LANES, LANES)
        return [
            pltpu.make_async_copy(ref.at[:, lanes], columns.at[p, n], sems.at[p, n])
            for n, ref in enumerate((q_hbm, k_hbm, v_hbm))
        ]

    for p in range(pairs):
        start_all(fetch(p))
    width = w_own_ref.shape[1]
    mine = pl.multiple_of(lax.axis_index("tp") * width, LANES)
    later = start_all([
        pltpu.make_async_copy(w_hbm.at[:, pl.ds(mine, width)], w_own_ref, more_sems.at[0]),
        pltpu.make_async_copy(r_hbm.at[pl.ds(WIN, blocks * WIN), :], r_in_ref, more_sems.at[1]),
    ])
    values[0, :, LANES:], values[1, :, LANES:] = split_heads(jnp.ones((frames, LANES), jnp.bfloat16))
    for i in range(blocks):
        def store(top, count, left, value):
            bias[i, top : top + count, left : left + LANES] = value

        band_bias(anchor + (i + 1) * WIN, WIN, anchor + i * WIN, span, starts_ref, lengths_ref, store)

    def one_pair(p, carry):
        lanes = pl.ds(pl.multiple_of(p * LANES, LANES), LANES)
        for n, ref in enumerate((q_hbm, k_hbm, v_hbm)):
            pltpu.make_async_copy(ref.at[:, lanes], columns.at[p, n], sems.at[p, n]).wait()
        keys[0], keys[1] = split_heads(columns[p, 1])
        values[0, :, :LANES], values[1, :, :LANES] = split_heads(columns[p, 2])
        for i in range(blocks):
            window = slice(i * WIN, i * WIN + span)
            both = jnp.concatenate([keys[0, window, :], keys[1, window, :]], axis=0)
            scores = lax.dot_general(
                columns[p, 0, (i + 1) * WIN : (i + 2) * WIN, :], both, (((1,), (1,)), ((), ())),
                preferred_element_type=jnp.float32,
            )
            weights = []
            for h in range(2):
                part = scores[:, h * span : (h + 1) * span] + bias[i]
                row_max = jnp.max(part, axis=1, keepdims=True)
                weights.append(jnp.exp2((part - row_max) * EXP_SCALE).astype(jnp.bfloat16))
            mixed = jnp.dot(
                jnp.concatenate(weights, axis=1),
                jnp.concatenate([values[0, window, :], values[1, window, :]], axis=0),
                preferred_element_type=jnp.float32,
            )
            mixed = jnp.where(bias_any(bias[i]), mixed[:, :LANES] / mixed[:, LANES:], 0.0)
            o_ref[i * WIN : (i + 1) * WIN, lanes] = mixed.astype(jnp.bfloat16)
        return carry

    lax.fori_loop(0, pairs, one_pair, 0)
    wait_all(later)


def halo_side():
    return 1 - lax.axis_index("seq") % 2


def attend_ends(
    frames, starts_ref, lengths_ref, q_hbm, k_hbm, v_hbm, first_hbm, second_hbm, o_ref, bias, query, keys, values, sems
):
    anchor = lax.axis_index("seq") * frames
    own = SPAN - REACH
    pairs = q_hbm.shape[1] // LANES
    side = halo_side()
    copies = []

    def move(source, target):
        copies.append(pltpu.make_async_copy(source, target, sems.at[len(copies)]))

    for target, ref, at, rows, mine in (
        (query, q_hbm, 2 * EDGE, EDGE, WIN), (keys, k_hbm, 3 * EDGE, REACH, own), (values, v_hbm, 3 * EDGE + REACH, REACH, own)
    ):
        move(ref.at[pl.ds(0, mine), :], target.at[0, pl.ds(rows, mine), :])
        move(ref.at[pl.ds(frames - mine, mine), :], target.at[1, pl.ds(0, mine), :])
        for halo, which in ((first_hbm, side), (second_hbm, 1 - side)):
            top = pl.multiple_of(which * mine, EDGE)
            move(halo.at[pl.ds(at, rows), :], target.at[which, pl.ds(top, rows), :])
    start_all(copies)
    for i, (base, key_base) in enumerate(((-EDGE, -REACH), (frames - WIN, frames - own))):
        def store(top, count, left, value):
            bias[i, top : top + count, left : left + LANES] = value

        band_bias(anchor + base, REACH, anchor + key_base, SPAN, starts_ref, lengths_ref, store)
    wait_all(copies)
    ones = jnp.ones((SPAN, LANES), jnp.bfloat16)

    def one_pair(p, carry):
        lanes = pl.ds(pl.multiple_of(p * LANES, LANES), LANES)
        for i in range(2):
            o_ref[i * REACH : (i + 1) * REACH, lanes] = head_pair(
                query[i, :, lanes], keys[i, :, lanes], jnp.concatenate([values[i, :, lanes], ones], axis=1), bias[i]
            )
        return carry

    lax.fori_loop(0, pairs, one_pair, 0, unroll=2)


def pack_edges(frames, q_ref, k_ref, v_ref, r_ref, w_ref, first_ref, second_ref, w_send_ref, sems):
    half = q_ref.shape[1]
    odd = lax.axis_index("seq") % 2
    copies = []
    for i, out in enumerate((first_ref, second_ref)):
        bottom = (1 - odd) if i == 0 else odd

        def rows(ref, n, left=0):
            return ref.at[pl.ds(pl.multiple_of(bottom * (frames - n), EDGE), n), pl.ds(left, half)]

        moves = [
            (rows(r_ref, EDGE), 0, EDGE),
            (rows(r_ref, EDGE, half), EDGE, EDGE),
            (rows(q_ref, EDGE), 2 * EDGE, EDGE),
            (rows(k_ref, REACH), 3 * EDGE, REACH),
            (rows(v_ref, REACH), 3 * EDGE + REACH, REACH),
        ]
        for n, (source, at, count) in enumerate(moves):
            copies.append(pltpu.make_async_copy(source, out.at[pl.ds(at, count), :], sems.at[i, n]))
    width = w_send_ref.shape[1]
    left = pl.multiple_of((1 - lax.axis_index("tp")) * width, LANES)
    copies.append(pltpu.make_async_copy(w_ref.at[:, pl.ds(left, width)], w_send_ref, sems.at[2, 0]))
    wait_all(start_all(copies))


def project(
    inner, own_hbm, other_hbm, w_own_hbm, w_other_hbm, r_hbm, first_hbm, second_hbm,
    h_ref, stats_ref, left, right, residual, shift, first, second, sems,
):
    rows, width = h_ref.shape
    half = own_hbm.shape[1]
    step = 256
    copies = []

    def move(source, target):
        copies.append(pltpu.make_async_copy(source, target, sems.at[len(copies)]))

    move(own_hbm, left.at[:, pl.ds(0, half)])
    move(w_own_hbm, right.at[pl.ds(0, half), :])
    move(other_hbm, left.at[:, pl.ds(half, half)])
    move(w_other_hbm, right.at[pl.ds(half, half), :])
    if inner:
        move(r_hbm, residual)
    else:
        frames = r_hbm.shape[0]
        move(r_hbm.at[pl.ds(0, WIN), :], residual.at[pl.ds(EDGE, WIN), :])
        move(r_hbm.at[pl.ds(frames - WIN, WIN), :], residual.at[pl.ds(REACH, WIN), :])
        side = halo_side()
        for halo, which in ((first_hbm, side), (second_hbm, 1 - side)):
            at = pl.ds(pl.multiple_of(which * (REACH + WIN), EDGE), EDGE)
            for n in range(2):
                move(halo.at[pl.ds(n * EDGE, EDGE), :], residual.at[at, pl.ds(n * half, half)])
    wait_all(start_all(copies))

    def gather(j):
        first_sum, second_sum = first[...], second[...]
        for l in range(j * step, (j + 1) * step, LANES):
            off = h_ref[:, l : l + LANES] - shift[...]
            first_sum = first_sum + off
            second_sum = second_sum + off * off
        first[...] = first_sum
        second[...] = second_sum

    first[...] = jnp.zeros_like(first)
    second[...] = jnp.zeros_like(second)
    for j in range(width // step):
        cols = slice(j * step, (j + 1) * step)
        part = jnp.dot(left[...], right[:, cols], preferred_element_type=jnp.float32)
        h_ref[:, cols] = part + residual[:, cols].astype(jnp.float32)
        if j == 0:
            mean = jnp.sum(h_ref[:, cols], axis=1, keepdims=True) * (1.0 / step)
            shift[...] = jnp.broadcast_to(mean, (rows, LANES))
        else:
            gather(j - 1)
    gather(width // step - 1)
    moved = jnp.sum(first[...], axis=1, keepdims=True) * (1.0 / width)
    mean = shift[...] + moved
    square = jnp.sum(second[...], axis=1, keepdims=True) - moved * moved * float(width)
    for top in range(0, rows, LANES):
        count = min(LANES, rows - top)
        for k, column in enumerate((mean, jnp.broadcast_to(square, (rows, LANES)))):
            tile = column[top : top + count]
            if count < LANES:
                tile = jnp.concatenate([tile, jnp.zeros((LANES - count, LANES), jnp.float32)], axis=0)
            stats_ref[8 * k : 8 * k + 8, top : top + LANES] = jnp.transpose(tile)[:8, :]


def stat_columns(base, own, other, width, starts_ref, lengths_ref):
    positions = base + lax.broadcasted_iota(jnp.int32, (1, LANES), 1)
    index = jnp.zeros((1, LANES), jnp.int32) - 1
    for r in range(REC):
        start = starts_ref[r]
        inside = (positions >= start) & (positions < start + lengths_ref[r])
        index = jnp.where(inside, r, index)
    gap = own[0:1, :] - other[0:1, :]
    middle = 0.5 * (own[0:1, :] + other[0:1, :])
    var = (own[8:9, :] + other[8:9, :] + gap * gap * (width * 0.25)) * (1.0 / width)
    inverse = jnp.where(index >= 0, lax.rsqrt(var + 1e-5), 0.0)
    parity = jnp.where(index >= 0, (index % 2).astype(jnp.float32), -1.0)
    halves = jnp.where(index >= 0, 0.5, 0.0)
    return as_column(middle), as_column(inverse), as_column(parity), as_column(halves)


def mark_mixed(base, chunks, flags, at, starts_ref, lengths_ref):
    flags[at] = jnp.int32(0)
    for r in range(REC - 1):
        end, start = starts_ref[r] + lengths_ref[r], starts_ref[r + 1]
        low = jnp.maximum((end - KHALF - base) >> 4, 0)
        high = jnp.minimum((start + KHALF - base + EDGE - 1) >> 4, chunks)

        @pl.when(start - end < KHALF)
        def _():
            def add(c, carry):
                known = flags[at]
                flags[at + 1 + known] = c
                flags[at] = known + 1
                return carry

            lax.fori_loop(low, high, add, 0)


def convolve(load, w_ref):
    acc = load(0) * w_ref[0:1, :]
    for tap in range(1, KERNEL):
        acc = acc + load(tap) * w_ref[tap : tap + 1, :]
    return acc


def differences(x_ref, diffs):
    rows = x_ref.shape[0]
    x = x_ref[...]
    near = x[: rows - 8] - x[8:]
    diffs[0, : rows - 8, :] = near
    diffs[1, : rows - 16, :] = x[: rows - 16] - x[16:]
    diffs[2, : rows - 24, :] = near[: rows - 24] - near[16:]


def tap_sums(w_ref, wq):
    padded = jnp.concatenate([jnp.zeros((1, LANES), jnp.float32), w_ref[...]], axis=0)
    w0, w1, w2, w3 = (padded[8 * j : 8 * j + 8] for j in range(4))
    for n, value in enumerate((w0, w0 + w1, -w1, w0 + w2, w0 + w1 + w2 + w3, -(w1 + w3), -w2, -(w2 + w3), w3)):
        wq[n] = value


def conv_groups(x_ref, diffs, wq, ats):
    sources = (
        (diffs.at[2], 0), (diffs.at[1], 8), (diffs.at[2], 8),
        (diffs.at[0], 16), (x_ref, 24), (diffs.at[0], 24),
        (diffs.at[2], 16), (diffs.at[1], 24), (diffs.at[2], 24),
    )
    sums = [[None] * 9 for _ in ats]
    for s in range(8):
        for n, (ref, off) in enumerate(sources):
            weight = jnp.broadcast_to(wq[n, s : s + 1, :], (8, LANES))
            for group, at in zip(sums, ats):
                first = at - EDGE + s + off
                term = ref[first : first + 8, :] * weight
                group[n] = term if group[n] is None else group[n] + term
    results = []
    for t in sums:
        a0, a1 = t[1] + t[0], t[1] + t[2]
        p0, p1 = t[4] + t[3], t[4] + t[5]
        c0, c1 = t[7] + t[6], t[7] + t[8]
        results.append(jnp.concatenate([a0 + p0, a1 + p1, p0 + c0, p1 + c1], axis=0))
    return results


def silu_add(hidden, half):
    return (hidden + (half + half * jnp.tanh(half))).astype(jnp.bfloat16)


def conv_rows(rows, hidden, normed, parity, halves, diffs, wq, masked, flags, flag_at, w_ref, out):
    differences(normed, diffs)
    group = 2 * EDGE
    tops = list(range(0, rows - group, group)) + [rows - group]
    for start in range(0, len(tops), SHARE):
        some = tops[start : start + SHARE]
        for top, conv_sum in zip(some, conv_groups(normed, diffs, wq, [top + EDGE for top in some])):
            at = top + EDGE
            here = slice(at, at + group)
            out[top : top + group, :] = silu_add(hidden[here, :], conv_sum * halves[here, :])

    def again(c, carry):
        top = pl.multiple_of(flags[flag_at + 1 + c] * EDGE, EDGE)
        around, here = pl.ds(top, 3 * EDGE), pl.ds(top + EDGE, EDGE)
        conv_sum = jnp.zeros((EDGE, LANES), jnp.float32)
        for side in range(2):
            masked[...] = jnp.where(parity[around, :] == side, normed[around, :], 0.0)
            first = EDGE - KHALF
            part = convolve(lambda tap: masked[first + tap : first + tap + EDGE, :], w_ref)
            conv_sum = jnp.where(parity[here, :] == side, part, conv_sum)
        out[pl.ds(top, EDGE), :] = silu_add(hidden[here, :], conv_sum * 0.5)
        return carry

    lax.fori_loop(0, flags[flag_at], again, 0)


def norm_conv_inner(
    frames, starts_ref, lengths_ref, h_ref, own_ref, other_ref, gain_ref, w_ref, o_ref,
    mean, scale, parity, halves, normed, diffs, wq, masked, out, flags, sems,
):
    step, steps = pl.program_id(0), pl.num_programs(0)
    rows = frames - 2 * WIN
    kept = rows - 2 * EDGE
    base = lax.axis_index("seq") * frames + WIN

    @pl.when(step == 0)
    def _():
        width = 2.0 * LANES * steps
        for top in range(0, rows, LANES):
            here = slice(top, top + LANES)
            mean[here, :], scale[here, :], parity[here, :], halves[here, :] = stat_columns(
                base + top, own_ref[:, here], other_ref[:, here], width, starts_ref, lengths_ref
            )
        mark_mixed(base + EDGE, kept // EDGE, flags, 0, starts_ref, lengths_ref)

    value = (h_ref[...] - mean[...]) * scale[...] * gain_ref[...]
    normed[...] = value.astype(jnp.bfloat16).astype(jnp.float32)
    slot = step % 2

    def copy(at, which):
        return pltpu.make_async_copy(
            out.at[which], o_ref.at[pl.ds(WIN + EDGE, kept), pl.ds(pl.multiple_of(at * LANES, LANES), LANES)], sems.at[which]
        )

    @pl.when(step >= 2)
    def _():
        copy(step - 2, slot).wait()

    tap_sums(w_ref, wq)
    conv_rows(kept, h_ref, normed, parity, halves, diffs, wq, masked, flags, 0, w_ref, out.at[slot])
    copy(step, slot).start()

    @pl.when(step == steps - 1)
    def _():
        copy(step - 1, 1 - slot).wait()
        copy(step, slot).wait()


def norm_conv_ends(
    frames, starts_ref, lengths_ref, h_end_ref, h_low_ref, h_high_ref, s_end_ref, t_end_ref, s_in_ref, t_in_ref,
    gain_ref, w_ref, done_ref, o_ref, mean, scale, parity, halves, hidden, normed, diffs, wq, masked, out, flags, sems,
):
    step, steps = pl.program_id(0), pl.num_programs(0)
    inner = frames - 2 * WIN
    anchor = lax.axis_index("seq") * frames
    more = 2 * EDGE
    rows = REACH + more

    @pl.when(step == 0)
    def _():
        width = 2.0 * LANES * steps

        def place(i, at, count, base, lane, own, other, skip):
            values = stat_columns(
                base, own[:, lane : lane + LANES], other[:, lane : lane + LANES], width, starts_ref, lengths_ref
            )
            for ref, value in zip((mean, scale, parity, halves), values):
                ref[i, at : at + count, :] = value[skip : skip + count]

        for top, count in ((0, LANES), (LANES, EDGE)):
            place(0, top, count, anchor - EDGE + top, top, s_end_ref, t_end_ref, 0)
        place(0, REACH, more, anchor + WIN, 0, s_in_ref, t_in_ref, 0)
        place(1, 0, more, anchor + frames - 2 * WIN, inner - LANES, s_in_ref, t_in_ref, LANES - more)
        own = jnp.concatenate([s_end_ref[:, LANES : 2 * LANES], s_end_ref[:, 2 * LANES :]], axis=1)[:, EDGE : EDGE + 2 * LANES - EDGE]
        other = jnp.concatenate([t_end_ref[:, LANES : 2 * LANES], t_end_ref[:, 2 * LANES :]], axis=1)[:, EDGE : EDGE + 2 * LANES - EDGE]
        place(1, more, LANES, anchor + frames - WIN, 0, own, other, 0)
        tail = jnp.concatenate([s_end_ref[:, 2 * LANES + EDGE :], jnp.zeros((16, LANES), jnp.float32)], axis=1)
        tail2 = jnp.concatenate([t_end_ref[:, 2 * LANES + EDGE :], jnp.zeros((16, LANES), jnp.float32)], axis=1)
        place(1, more + LANES, EDGE, anchor + frames, 0, tail, tail2, 0)
        for i in range(2):
            mark_mixed(anchor + i * (frames - REACH), REACH // EDGE, flags, i * 64, starts_ref, lengths_ref)

    hidden[0, :REACH, :] = h_end_ref[:REACH, :]
    hidden[0, REACH:, :] = h_low_ref[...]
    hidden[1, :more, :] = h_high_ref[...]
    hidden[1, more:, :] = h_end_ref[REACH:, :]
    slot = step % 2

    def copies(at, which):
        lanes = pl.ds(pl.multiple_of(at * LANES, LANES), LANES)
        return [
            pltpu.make_async_copy(
                out.at[which, i], o_ref.at[pl.ds(i * (frames - REACH), REACH), lanes], sems.at[which, i]
            )
            for i in range(2)
        ]

    @pl.when(step >= 2)
    def _():
        for copy in copies(step - 2, slot):
            copy.wait()

    tap_sums(w_ref, wq)
    for i in range(2):
        value = (hidden[i] - mean[i]) * scale[i] * gain_ref[...]
        normed[i] = value.astype(jnp.bfloat16).astype(jnp.float32)
        conv_rows(
            REACH, hidden.at[i], normed.at[i], parity.at[i], halves.at[i], diffs.at[i], wq, masked, flags, i * 64, w_ref,
            out.at[slot, i],
        )
    for copy in copies(step, slot):
        copy.start()

    @pl.when(step == steps - 1)
    def _():
        for copy in copies(step - 1, 1 - slot) + copies(step, slot):
            copy.wait()


def cost(microseconds):
    return pl.CostEstimate(flops=int(microseconds * 4e8), bytes_accessed=1000, transcendentals=0)


def params(mebibytes):
    return pltpu.CompilerParams(vmem_limit_bytes=mebibytes * 2**20)


def on_device(
    queries, attn_keys, attn_values, out_weight, residual, norm_gain, conv_weight, record_starts, record_lengths
):
    frames, heads_width = queries.shape
    width = residual.shape[1]
    pairs = heads_width // LANES
    inner = frames - 2 * WIN
    ends = 2 * REACH
    count = lax.axis_size("seq")
    swap = [(0, 1), (1, 0)]
    anywhere = pl.BlockSpec(memory_space=pl.ANY)

    edges = jax.ShapeDtypeStruct((3 * EDGE + 2 * REACH, heads_width), jnp.bfloat16)
    halved = jax.ShapeDtypeStruct((heads_width, width), jnp.bfloat16)
    first_edge, second_edge, weight_send = pl.pallas_call(
        functools.partial(pack_edges, frames),
        out_shape=[edges, edges, halved],
        in_specs=[pl.BlockSpec(memory_space=pltpu.HBM)] * 5,
        out_specs=[pl.BlockSpec(memory_space=pltpu.VMEM)] * 3,
        scratch_shapes=[pltpu.SemaphoreType.DMA((3, 5))],
        compiler_params=params(52),
        name="pack_edges",
    )(queries, attn_keys, attn_values, residual, out_weight)
    first_edge, second_edge, queries = lax.optimization_barrier((first_edge, second_edge, queries))
    first = lax.ppermute(first_edge, "seq", [(i, i ^ 1) for i in range(count)])
    second = lax.ppermute(second_edge, "seq", [(i, ((i + 1) ^ 1) - 1) for i in range(1, count - 1)])
    weight_other = lax.ppermute(weight_send, "tp", swap)

    hbm = pl.BlockSpec(memory_space=pltpu.HBM)
    vmem = pl.BlockSpec(memory_space=pltpu.VMEM)
    attended_in, weight_own, residual_in = pl.pallas_call(
        functools.partial(attend_inner, frames),
        out_shape=[
            jax.ShapeDtypeStruct((inner, heads_width), jnp.bfloat16), halved,
            jax.ShapeDtypeStruct((inner, width), jnp.bfloat16),
        ],
        in_specs=[SMEM, SMEM, hbm, hbm, hbm, hbm, hbm],
        out_specs=[vmem, vmem, vmem],
        scratch_shapes=[
            pltpu.VMEM((pairs, 3, frames, LANES), jnp.bfloat16),
            pltpu.VMEM((inner // WIN, WIN, 3 * WIN), jnp.float32),
            pltpu.VMEM((2, frames, LANES), jnp.bfloat16),
            pltpu.VMEM((2, frames, 2 * LANES), jnp.bfloat16),
            pltpu.SemaphoreType.DMA((pairs, 3)),
            pltpu.SemaphoreType.DMA((2,)),
        ],
        compiler_params=params(42),
        cost_estimate=cost(0.2),
        name="attend_inner",
    )(record_starts, record_lengths, queries, attn_keys, attn_values, out_weight, residual)

    def projection(inside, own, other, microseconds, name):
        rows = own.shape[0]
        padded = -(-rows // LANES) * LANES
        shared = pltpu.VMEM((rows, LANES), jnp.float32)
        halos = [first_edge, second_edge] if inside else [first, second]
        return pl.pallas_call(
            functools.partial(project, inside),
            in_specs=[anywhere] * 7,
            out_specs=[vmem, vmem],
            scratch_shapes=[
                pltpu.VMEM((rows, 2 * heads_width), jnp.bfloat16),
                pltpu.VMEM((2 * heads_width, width), jnp.bfloat16),
                pltpu.VMEM((rows, width), jnp.bfloat16),
                shared, shared, shared,
                pltpu.SemaphoreType.DMA((10,)),
            ],
            out_shape=[
                jax.ShapeDtypeStruct((rows, width), jnp.float32),
                jax.ShapeDtypeStruct((16, padded), jnp.float32),
            ],
            compiler_params=params(24),
            cost_estimate=cost(microseconds),
            name=name,
        )(own, other, weight_own, weight_other, residual_in if inside else residual, *halos)

    other_in = lax.ppermute(attended_in, "tp", swap)
    hidden_in, stats_in = projection(True, attended_in, other_in, 0.2, "project_inner")
    other_stats_in = lax.ppermute(stats_in, "tp", swap)

    whole = lambda array: pl.BlockSpec(array.shape, lambda g: (0, 0))
    lane_block = lambda n, i=0: pl.BlockSpec((n, LANES), lambda g: (i, g))
    gain = norm_gain.reshape(1, width)
    shared = lambda n: pltpu.VMEM(n + (LANES,), jnp.float32)
    kept = inner - 2 * EDGE
    result = jax.ShapeDtypeStruct((frames, width), jnp.bfloat16)
    partly = pl.pallas_call(
        functools.partial(norm_conv_inner, frames),
        grid=(width // LANES,),
        out_shape=result,
        in_specs=[SMEM, SMEM, lane_block(inner), whole(stats_in), whole(stats_in), lane_block(1), lane_block(KERNEL)],
        out_specs=anywhere,
        scratch_shapes=[
            shared((inner,)), shared((inner,)), shared((inner,)), shared((inner,)), shared((inner,)), shared((3, inner)), shared((9, 8)),
            shared((3 * EDGE,)),
            pltpu.VMEM((2, kept, LANES), jnp.bfloat16),
            pltpu.SMEM((64,), jnp.int32),
            pltpu.SemaphoreType.DMA((2,)),
        ],
        compiler_params=params(16),
        cost_estimate=cost(0.2),
        name="norm_conv_inner",
    )(record_starts, record_lengths, hidden_in, stats_in, other_stats_in, gain, conv_weight)

    first, second, partly = lax.optimization_barrier((first, second, partly))
    wide = lambda n: pltpu.VMEM((2, n, heads_width), jnp.bfloat16)
    attended_end = pl.pallas_call(
        functools.partial(attend_ends, frames),
        out_shape=jax.ShapeDtypeStruct((ends, heads_width), jnp.bfloat16),
        in_specs=[SMEM, SMEM, hbm, hbm, hbm, anywhere, anywhere],
        out_specs=vmem,
        scratch_shapes=[
            pltpu.VMEM((2, REACH, SPAN), jnp.float32), wide(REACH), wide(SPAN), wide(SPAN), pltpu.SemaphoreType.DMA((12,)),
        ],
        compiler_params=params(16),
        cost_estimate=cost(5),
        name="attend_ends",
    )(record_starts, record_lengths, queries, attn_keys, attn_values, first, second)

    other_end = lax.ppermute(attended_end, "tp", swap)
    hidden_end, stats_end = projection(False, attended_end, other_end, 4, "project_ends")
    other_stats_end = lax.ppermute(stats_end, "tp", swap)

    more = 2 * EDGE
    rows = REACH + more
    return pl.pallas_call(
        functools.partial(norm_conv_ends, frames),
        grid=(width // LANES,),
        out_shape=result,
        in_specs=[
            SMEM, SMEM, lane_block(ends), lane_block(more), lane_block(more, inner // more - 1),
            whole(stats_end), whole(stats_end), whole(stats_in), whole(stats_in), lane_block(1), lane_block(KERNEL),
            anywhere,
        ],
        out_specs=anywhere,
        scratch_shapes=[
            shared((2, rows)), shared((2, rows)), shared((2, rows)), shared((2, rows)), shared((2, rows)), shared((2, rows)),
            shared((2, 3, rows)), shared((9, 8)), shared((3 * EDGE,)),
            pltpu.VMEM((2, 2, REACH, LANES), jnp.bfloat16),
            pltpu.SMEM((128,), jnp.int32),
            pltpu.SemaphoreType.DMA((2, 2)),
        ],
        input_output_aliases={11: 0},
        compiler_params=params(16),
        cost_estimate=cost(5),
        name="norm_conv_ends",
    )(
        record_starts, record_lengths, hidden_end, hidden_in, hidden_in, stats_end, other_stats_end, stats_in,
        other_stats_in, gain, conv_weight, partly,
    )


def solution(mesh):
    placed = (
        P(("grp", "seq"), "tp"),
        P(("grp", "seq"), "tp"),
        P(("grp", "seq"), "tp"),
        P("tp", None),
        P(("grp", "seq"), "tp"),
        P("tp"),
        P(None, "tp"),
        P("grp"),
        P("grp"),
    )
    return jax.shard_map(
        on_device, mesh=mesh, in_specs=placed, out_specs=P(("grp", "seq"), "tp"), check_vma=False
    )
```

```python
import functools

import jax
import jax.numpy as jnp
from jax import lax
from jax.experimental import pallas as pl
from jax.experimental.pallas import tpu as pltpu
from jax.sharding import PartitionSpec as P

D = 3072
HSIZE = 64
WIN = 128
KHALF = 15
REC = 8
KERNEL = 31
EDGE = 16
REACH = WIN + EDGE
SPAN = 512
LANES = 128
NEG = -1e30
SHARE = 4
EXP_SCALE = HSIZE ** (-0.5) * 1.4426950408889634
SMEM = pl.BlockSpec(memory_space=pltpu.SMEM)


def row_bounds(positions, starts_ref, lengths_ref):
    first = jnp.full(positions.shape, -1, jnp.int32)
    last = jnp.full(positions.shape, -2, jnp.int32)
    for r in range(REC):
        start = starts_ref[r]
        end = start + lengths_ref[r]
        inside = (positions >= start) & (positions < end)
        first = jnp.where(inside, start, first)
        last = jnp.where(inside, end - 1, last)
    return first, last


def as_column(row):
    return jnp.transpose(jnp.broadcast_to(row, (LANES, LANES)))


def band_bias(base, rows, key_base, keys, starts_ref, lengths_ref, store):
    for top in range(0, rows, LANES):
        count = min(LANES, rows - top)
        positions = base + top + lax.broadcasted_iota(jnp.int32, (1, LANES), 1)
        first, last = row_bounds(positions, starts_ref, lengths_ref)
        inside = first >= 0
        low = jnp.where(inside, jnp.maximum(first, positions - WIN), 0)
        high = jnp.where(inside, jnp.minimum(last, positions + WIN), -1)
        low = as_column(low.astype(jnp.float32))
        high = as_column(high.astype(jnp.float32))
        for left in range(0, keys, LANES):
            key_at = (key_base + left + lax.broadcasted_iota(jnp.int32, (LANES, LANES), 1)).astype(jnp.float32)
            bias = jnp.where((key_at >= low) & (key_at <= high), jnp.float32(0.0), jnp.float32(NEG))
            store(top, count, left, bias[:count])


def head_pair(query, keys, values, bias):
    span = bias.shape[1]
    scores = lax.dot_general(query, keys, (((1,), (1,)), ((), ())), preferred_element_type=jnp.float32)
    weights = []
    for h in range(2):
        part = scores[:, h * span : (h + 1) * span] + bias
        row_max = jnp.max(part, axis=1, keepdims=True)
        weights.append(jnp.exp2((part - row_max) * EXP_SCALE).astype(jnp.bfloat16))
    mixed = jnp.dot(jnp.concatenate(weights, axis=1), values, preferred_element_type=jnp.float32)
    return jnp.where(bias_any(bias), mixed[:, :LANES] / mixed[:, LANES:], 0.0).astype(jnp.bfloat16)


def bias_any(bias):
    return jnp.max(bias, axis=1, keepdims=True) > NEG / 2


def split_heads(array):
    left = lax.broadcasted_iota(jnp.int32, array.shape, 1) < HSIZE
    nothing = jnp.zeros_like(array)
    return jnp.where(left, array, nothing), jnp.where(left, nothing, array)


def start_all(copies):
    for copy in copies:
        copy.start()
    return copies


def wait_all(copies):
    for copy in copies:
        copy.wait()


def attend_inner(
    frames, starts_ref, lengths_ref, q_hbm, k_hbm, v_hbm, w_hbm, r_hbm, o_ref, w_own_ref, r_in_ref,
    columns, bias, keys, values, sems, more_sems
):
    blocks = frames // WIN - 2
    span = 3 * WIN
    pairs = q_hbm.shape[1] // LANES
    anchor = lax.axis_index("seq") * frames

    def fetch(p):
        lanes = pl.ds(p * LANES, LANES)
        return [
            pltpu.make_async_copy(ref.at[:, lanes], columns.at[p, n], sems.at[p, n])
            for n, ref in enumerate((q_hbm, k_hbm, v_hbm))
        ]

    for p in range(pairs):
        start_all(fetch(p))
    width = w_own_ref.shape[1]
    mine = pl.multiple_of(lax.axis_index("tp") * width, LANES)
    later = start_all([
        pltpu.make_async_copy(w_hbm.at[:, pl.ds(mine, width)], w_own_ref, more_sems.at[0]),
        pltpu.make_async_copy(r_hbm.at[pl.ds(WIN, blocks * WIN), :], r_in_ref, more_sems.at[1]),
    ])
    values[0, :, LANES:], values[1, :, LANES:] = split_heads(jnp.ones((frames, LANES), jnp.bfloat16))
    for i in range(blocks):
        def store(top, count, left, value):
            bias[i, top : top + count, left : left + LANES] = value

        band_bias(anchor + (i + 1) * WIN, WIN, anchor + i * WIN, span, starts_ref, lengths_ref, store)

    def one_pair(p, carry):
        lanes = pl.ds(pl.multiple_of(p * LANES, LANES), LANES)
        for n, ref in enumerate((q_hbm, k_hbm, v_hbm)):
            pltpu.make_async_copy(ref.at[:, lanes], columns.at[p, n], sems.at[p, n]).wait()
        keys[0], keys[1] = split_heads(columns[p, 1])
        values[0, :, :LANES], values[1, :, :LANES] = split_heads(columns[p, 2])
        for i in range(blocks):
            window = slice(i * WIN, i * WIN + span)
            o_ref[i * WIN : (i + 1) * WIN, lanes] = head_pair(
                columns[p, 0, (i + 1) * WIN : (i + 2) * WIN, :],
                jnp.concatenate([keys[0, window, :], keys[1, window, :]], axis=0),
                jnp.concatenate([values[0, window, :], values[1, window, :]], axis=0),
                bias[i],
            )
        return carry

    lax.fori_loop(0, pairs, one_pair, 0)
    wait_all(later)


def halo_side():
    return 1 - lax.axis_index("seq") % 2


def attend_ends(
    frames, starts_ref, lengths_ref, q_hbm, k_hbm, v_hbm, first_hbm, second_hbm, o_ref, bias, query, keys, values, sems
):
    anchor = lax.axis_index("seq") * frames
    own = SPAN - REACH
    pairs = q_hbm.shape[1] // LANES
    side = halo_side()
    copies = []

    def move(source, target):
        copies.append(pltpu.make_async_copy(source, target, sems.at[len(copies)]))

    for target, ref, at, rows, mine in (
        (query, q_hbm, 2 * EDGE, EDGE, WIN), (keys, k_hbm, 3 * EDGE, REACH, own), (values, v_hbm, 3 * EDGE + REACH, REACH, own)
    ):
        move(ref.at[pl.ds(0, mine), :], target.at[0, pl.ds(rows, mine), :])
        move(ref.at[pl.ds(frames - mine, mine), :], target.at[1, pl.ds(0, mine), :])
        for halo, which in ((first_hbm, side), (second_hbm, 1 - side)):
            top = pl.multiple_of(which * mine, EDGE)
            move(halo.at[pl.ds(at, rows), :], target.at[which, pl.ds(top, rows), :])
    start_all(copies)
    for i, (base, key_base) in enumerate(((-EDGE, -REACH), (frames - WIN, frames - own))):
        def store(top, count, left, value):
            bias[i, top : top + count, left : left + LANES] = value

        band_bias(anchor + base, REACH, anchor + key_base, SPAN, starts_ref, lengths_ref, store)
    wait_all(copies)
    ones = split_heads(jnp.ones((SPAN, LANES), jnp.bfloat16))
    for p in range(pairs):
        lanes = slice(p * LANES, (p + 1) * LANES)
        for i in range(2):
            sides = [jnp.concatenate([v, one], axis=1) for v, one in zip(split_heads(values[i, :, lanes]), ones)]
            o_ref[i * REACH : (i + 1) * REACH, lanes] = head_pair(
                query[i, :, lanes],
                jnp.concatenate(split_heads(keys[i, :, lanes]), axis=0),
                jnp.concatenate(sides, axis=0),
                bias[i],
            )


def pack_edges(frames, q_ref, k_ref, v_ref, r_ref, first_ref, second_ref, sems):
    half = q_ref.shape[1]
    odd = lax.axis_index("seq") % 2
    copies = []
    for i, out in enumerate((first_ref, second_ref)):
        bottom = (1 - odd) if i == 0 else odd

        def rows(ref, n, left=0):
            return ref.at[pl.ds(pl.multiple_of(bottom * (frames - n), EDGE), n), pl.ds(left, half)]

        moves = [
            (rows(r_ref, EDGE), 0, EDGE),
            (rows(r_ref, EDGE, half), EDGE, EDGE),
            (rows(q_ref, EDGE), 2 * EDGE, EDGE),
            (rows(k_ref, REACH), 3 * EDGE, REACH),
            (rows(v_ref, REACH), 3 * EDGE + REACH, REACH),
        ]
        for n, (source, at, count) in enumerate(moves):
            copies.append(pltpu.make_async_copy(source, out.at[pl.ds(at, count), :], sems.at[i, n]))
    wait_all(start_all(copies))


def project_own(own_ref, w_ref, r_ref, more_hbm, o_ref, more_ref, sem):
    step = 256
    width = more_ref.shape[1]
    left = pl.multiple_of(lax.axis_index("tp") * width, LANES)
    later = pltpu.make_async_copy(more_hbm.at[:, pl.ds(left, width)], more_ref, sem)
    later.start()
    for left in range(0, o_ref.shape[1], step):
        cols = slice(left, left + step)
        part = jnp.dot(own_ref[...], w_ref[:, cols], preferred_element_type=jnp.float32)
        o_ref[:, cols] = part + r_ref[:, cols].astype(jnp.float32)
    later.wait()


def project(inner, *refs):
    if inner:
        other_hbm, w_other_hbm, base, h_ref, stats_ref, left, right, shift, first, second, sems = refs
    else:
        (own_hbm, other_hbm, w_own_hbm, w_other_hbm, r_hbm, first_hbm, second_hbm,
         h_ref, stats_ref, left, right, base, shift, first, second, sems) = refs
    rows, width = h_ref.shape
    half = other_hbm.shape[1]
    step = 256
    copies = []

    def move(source, target):
        copies.append(pltpu.make_async_copy(source, target, sems.at[len(copies)]))

    at = left.shape[1] - half
    move(other_hbm, left.at[:, pl.ds(at, half)])
    move(w_other_hbm, right.at[pl.ds(at, half), :])
    if not inner:
        move(own_hbm, left.at[:, pl.ds(0, half)])
        move(w_own_hbm, right.at[pl.ds(0, half), :])
        frames = r_hbm.shape[0]
        move(r_hbm.at[pl.ds(0, WIN), :], base.at[pl.ds(EDGE, WIN), :])
        move(r_hbm.at[pl.ds(frames - WIN, WIN), :], base.at[pl.ds(REACH, WIN), :])
        side = halo_side()
        for halo, which in ((first_hbm, side), (second_hbm, 1 - side)):
            target = pl.ds(pl.multiple_of(which * (REACH + WIN), EDGE), EDGE)
            for n in range(2):
                move(halo.at[pl.ds(n * EDGE, EDGE), :], base.at[target, pl.ds(n * half, half)])
    wait_all(start_all(copies))

    def gather(j):
        first_sum, second_sum = first[...], second[...]
        for l in range(j * step, (j + 1) * step, LANES):
            off = h_ref[:, l : l + LANES] - shift[...]
            first_sum = first_sum + off
            second_sum = second_sum + off * off
        first[...] = first_sum
        second[...] = second_sum

    first[...] = jnp.zeros_like(first)
    second[...] = jnp.zeros_like(second)
    for j in range(width // step):
        cols = slice(j * step, (j + 1) * step)
        part = jnp.dot(left[...], right[:, cols], preferred_element_type=jnp.float32)
        h_ref[:, cols] = part + base[:, cols].astype(jnp.float32)
        if j == 0:
            mean = jnp.sum(h_ref[:, cols], axis=1, keepdims=True) * (1.0 / step)
            shift[...] = jnp.broadcast_to(mean, (rows, LANES))
        else:
            gather(j - 1)
    gather(width // step - 1)
    moved = jnp.sum(first[...], axis=1, keepdims=True) * (1.0 / width)
    mean = shift[...] + moved
    square = jnp.sum(second[...], axis=1, keepdims=True) - moved * moved * float(width)
    for top in range(0, rows, LANES):
        count = min(LANES, rows - top)
        for k, column in enumerate((mean, jnp.broadcast_to(square, (rows, LANES)))):
            tile = column[top : top + count]
            if count < LANES:
                tile = jnp.concatenate([tile, jnp.zeros((LANES - count, LANES), jnp.float32)], axis=0)
            stats_ref[8 * k : 8 * k + 8, top : top + LANES] = jnp.transpose(tile)[:8, :]


def recording_of(base, starts_ref, lengths_ref):
    positions = base + lax.broadcasted_iota(jnp.int32, (1, LANES), 1)
    index = jnp.zeros((1, LANES), jnp.int32) - 1
    for r in range(REC):
        start = starts_ref[r]
        inside = (positions >= start) & (positions < start + lengths_ref[r])
        index = jnp.where(inside, r, index)
    return index


def stat_columns(base, own, other, width, starts_ref, lengths_ref):
    inside = recording_of(base, starts_ref, lengths_ref) >= 0
    gap = own[0:1, :] - other[0:1, :]
    middle = 0.5 * (own[0:1, :] + other[0:1, :])
    var = (own[8:9, :] + other[8:9, :] + gap * gap * (width * 0.25)) * (1.0 / width)
    inverse = jnp.where(inside, lax.rsqrt(var + 1e-5), 0.0)
    deviation = as_column(inverse)
    return as_column(middle), deviation, jnp.where(deviation > 0, 0.5, 0.0)


def parity_column(base, starts_ref, lengths_ref):
    index = recording_of(base, starts_ref, lengths_ref)
    return as_column(jnp.where(index >= 0, (index % 2).astype(jnp.float32), -1.0))


def mark_mixed(base, chunks, flags, at, starts_ref, lengths_ref):
    flags[at] = jnp.int32(0)
    for r in range(REC - 1):
        end, start = starts_ref[r] + lengths_ref[r], starts_ref[r + 1]
        low = jnp.maximum((end - KHALF - base) >> 4, 0)
        high = jnp.minimum((start + KHALF - base + EDGE - 1) >> 4, chunks)

        @pl.when(start - end < KHALF)
        def _():
            def add(c, carry):
                known = flags[at]
                flags[at + 1 + known] = c
                flags[at] = known + 1
                return carry

            lax.fori_loop(low, high, add, 0)


def convolve(load, w_ref):
    acc = load(0) * w_ref[0:1, :]
    for tap in range(1, KERNEL):
        acc = acc + load(tap) * w_ref[tap : tap + 1, :]
    return acc


def differences(x_ref, diffs):
    rows = x_ref.shape[0]
    x = x_ref[...]
    near = x[: rows - 8] - x[8:]
    diffs[0, : rows - 8, :] = near
    diffs[1, : rows - 16, :] = x[: rows - 16] - x[16:]
    diffs[2, : rows - 24, :] = near[: rows - 24] - near[16:]


def tap_sums(w_ref, wq):
    padded = jnp.concatenate([jnp.zeros((1, LANES), jnp.float32), w_ref[...]], axis=0)
    w0, w1, w2, w3 = (padded[8 * j : 8 * j + 8] for j in range(4))
    for n, value in enumerate((w0, w0 + w1, -w1, w0 + w2, w0 + w1 + w2 + w3, -(w1 + w3), -w2, -(w2 + w3), w3)):
        wq[n] = value


def conv_groups(x_ref, diffs, wq, ats):
    sources = (
        (diffs.at[2], 0), (diffs.at[1], 8), (diffs.at[2], 8),
        (diffs.at[0], 16), (x_ref, 24), (diffs.at[0], 24),
        (diffs.at[2], 16), (diffs.at[1], 24), (diffs.at[2], 24),
    )
    sums = [[None] * 9 for _ in ats]
    for s in range(8):
        for n, (ref, off) in enumerate(sources):
            weight = jnp.broadcast_to(wq[n, s : s + 1, :], (8, LANES))
            for group, at in zip(sums, ats):
                first = at - EDGE + s + off
                term = ref[first : first + 8, :] * weight
                group[n] = term if group[n] is None else group[n] + term
    results = []
    for t in sums:
        a0, a1 = t[1] + t[0], t[1] + t[2]
        p0, p1 = t[4] + t[3], t[4] + t[5]
        c0, c1 = t[7] + t[6], t[7] + t[8]
        results.append(jnp.concatenate([a0 + p0, a1 + p1, p0 + c0, p1 + c1], axis=0))
    return results


def silu_add(hidden, half):
    return (hidden + (half + half * jnp.tanh(half))).astype(jnp.bfloat16)


def conv_rows(rows, hidden, normed, parity, halves, diffs, wq, masked, flags, flag_at, w_ref, out):
    differences(normed, diffs)
    tap_sums(w_ref, wq)
    group = 2 * EDGE
    tops = list(range(0, rows - group, group)) + [rows - group]
    for start in range(0, len(tops), SHARE):
        some = tops[start : start + SHARE]
        for top, conv_sum in zip(some, conv_groups(normed, diffs, wq, [top + EDGE for top in some])):
            at = top + EDGE
            here = slice(at, at + group)
            out[top : top + group, :] = silu_add(hidden[here, :], conv_sum * halves[here, :])

    def again(c, carry):
        top = pl.multiple_of(flags[flag_at + 1 + c] * EDGE, EDGE)
        around, here = pl.ds(top, 3 * EDGE), pl.ds(top + EDGE, EDGE)
        conv_sum = jnp.zeros((EDGE, LANES), jnp.float32)
        for side in range(2):
            masked[...] = jnp.where(parity[around, :] == side, normed[around, :], 0.0)
            first = EDGE - KHALF
            part = convolve(lambda tap: masked[first + tap : first + tap + EDGE, :], w_ref)
            conv_sum = jnp.where(parity[here, :] == side, part, conv_sum)
        out[pl.ds(top, EDGE), :] = silu_add(hidden[here, :], conv_sum * 0.5)
        return carry

    lax.fori_loop(0, flags[flag_at], again, 0)


def norm_conv_inner(
    frames, starts_ref, lengths_ref, h_ref, own_ref, other_ref, gain_ref, w_ref, o_ref,
    mean, scale, parity, halves, normed, diffs, wq, masked, out, flags, sems,
):
    step, steps = pl.program_id(0), pl.num_programs(0)
    rows, wide = h_ref.shape
    kept = rows - 2 * EDGE
    base = lax.axis_index("seq") * frames + WIN

    @pl.when(step == 0)
    def _():
        width = 2.0 * wide * steps
        mark_mixed(base + EDGE, kept // EDGE, flags, 0, starts_ref, lengths_ref)
        for top in range(0, rows, LANES):
            here = slice(top, top + LANES)
            mean[here, :], scale[here, :], halves[here, :] = stat_columns(
                base + top, own_ref[:, here], other_ref[:, here], width, starts_ref, lengths_ref
            )

        @pl.when(flags[0] > 0)
        def _():
            for top in range(0, rows, LANES):
                parity[top : top + LANES, :] = parity_column(base + top, starts_ref, lengths_ref)

    slot = step % 2

    def copy(at, which):
        lanes = pl.ds(pl.multiple_of(at * wide, LANES), wide)
        return pltpu.make_async_copy(out.at[which], o_ref.at[pl.ds(WIN + EDGE, kept), lanes], sems.at[which])

    @pl.when(step >= 2)
    def _():
        copy(step - 2, slot).wait()

    for u in range(wide // LANES):
        lanes = slice(u * LANES, (u + 1) * LANES)
        value = (h_ref[:, lanes] - mean[...]) * scale[...] * gain_ref[:, lanes]
        normed[u] = value.astype(jnp.bfloat16).astype(jnp.float32)
        conv_rows(
            kept, h_ref.at[:, lanes], normed.at[u], parity, halves, diffs.at[u], wq.at[u], masked, flags, 0,
            w_ref.at[:, lanes], out.at[slot, :, lanes],
        )
    copy(step, slot).start()

    @pl.when(step == steps - 1)
    def _():
        copy(step - 1, 1 - slot).wait()
        copy(step, slot).wait()


def norm_conv_ends(
    frames, starts_ref, lengths_ref, h_end_ref, h_low_ref, h_high_ref, s_end_ref, t_end_ref, s_in_ref, t_in_ref,
    gain_ref, w_ref, done_ref, o_ref, mean, scale, parity, halves, hidden, normed, diffs, wq, masked, out, flags, sems,
):
    step, steps = pl.program_id(0), pl.num_programs(0)
    inner = frames - 2 * WIN
    anchor = lax.axis_index("seq") * frames
    more = 2 * EDGE
    rows = REACH + more
    wide = h_end_ref.shape[1]

    @pl.when(step == 0)
    def _():
        width = 2.0 * wide * steps
        for i in range(2):
            mark_mixed(anchor + i * (frames - REACH), REACH // EDGE, flags, i * 64, starts_ref, lengths_ref)

        def joined(ends, ins, i):
            if i == 0:
                return jnp.concatenate([ends[:, :REACH], ins[:, : 2 * LANES - REACH]], axis=1)
            return jnp.concatenate([ins[:, inner - more :], ends[:, REACH : REACH + 2 * LANES - more]], axis=1)

        for i, first in enumerate((anchor - EDGE, anchor + frames - WIN - more)):
            own, other = joined(s_end_ref, s_in_ref, i), joined(t_end_ref, t_in_ref, i)
            for top, count in ((0, LANES), (LANES, rows - LANES)):
                here, lanes = slice(top, top + count), slice(top, top + LANES)
                values = stat_columns(first + top, own[:, lanes], other[:, lanes], width, starts_ref, lengths_ref)
                for ref, value in zip((mean, scale, halves), values):
                    ref[i, here, :] = value[:count]

                @pl.when(flags[0] + flags[64] > 0)
                def _():
                    parity[i, here, :] = parity_column(first + top, starts_ref, lengths_ref)[:count]

    slot = step % 2

    def copies(at, which):
        lanes = pl.ds(pl.multiple_of(at * wide, LANES), wide)
        return [
            pltpu.make_async_copy(
                out.at[which, i], o_ref.at[pl.ds(i * (frames - REACH), REACH), lanes], sems.at[which, i]
            )
            for i in range(2)
        ]

    @pl.when(step >= 2)
    def _():
        for copy in copies(step - 2, slot):
            copy.wait()

    for u in range(wide // LANES):
        lanes = slice(u * LANES, (u + 1) * LANES)
        hidden[u, 0, :REACH, :] = h_end_ref[:REACH, lanes]
        hidden[u, 0, REACH:, :] = h_low_ref[:, lanes]
        hidden[u, 1, :more, :] = h_high_ref[:, lanes]
        hidden[u, 1, more:, :] = h_end_ref[REACH:, lanes]
        for i in range(2):
            value = (hidden[u, i] - mean[i]) * scale[i] * gain_ref[:, lanes]
            normed[u, i] = value.astype(jnp.bfloat16).astype(jnp.float32)
            conv_rows(
                REACH, hidden.at[u, i], normed.at[u, i], parity.at[i], halves.at[i], diffs.at[u, i], wq.at[u], masked,
                flags, i * 64, w_ref.at[:, lanes], out.at[slot, i, :, lanes],
            )
    for copy in copies(step, slot):
        copy.start()

    @pl.when(step == steps - 1)
    def _():
        for copy in copies(step - 1, 1 - slot) + copies(step, slot):
            copy.wait()


def cost(microseconds):
    return pl.CostEstimate(flops=int(microseconds * 4e8), bytes_accessed=1000, transcendentals=0)


def params(mebibytes):
    return pltpu.CompilerParams(vmem_limit_bytes=mebibytes * 2**20)


def on_device(
    queries, attn_keys, attn_values, out_weight, residual, norm_gain, conv_weight, record_starts, record_lengths
):
    frames, heads_width = queries.shape
    width = residual.shape[1]
    pairs = heads_width // LANES
    inner = frames - 2 * WIN
    ends = 2 * REACH
    count = lax.axis_size("seq")
    swap = [(0, 1), (1, 0)]
    anywhere = pl.BlockSpec(memory_space=pl.ANY)

    edges = jax.ShapeDtypeStruct((3 * EDGE + 2 * REACH, heads_width), jnp.bfloat16)
    halved = jax.ShapeDtypeStruct((heads_width, width), jnp.bfloat16)
    first_edge, second_edge = pl.pallas_call(
        functools.partial(pack_edges, frames),
        out_shape=[edges, edges],
        in_specs=[pl.BlockSpec(memory_space=pltpu.HBM)] * 4,
        out_specs=[pl.BlockSpec(memory_space=pltpu.VMEM)] * 2,
        scratch_shapes=[pltpu.SemaphoreType.DMA((2, 5))],
        compiler_params=params(52),
        name="pack_edges",
    )(queries, attn_keys, attn_values, residual)
    first_edge, second_edge, queries = lax.optimization_barrier((first_edge, second_edge, queries))
    first = lax.ppermute(first_edge, "seq", [(i, i ^ 1) for i in range(count)])
    second = lax.ppermute(second_edge, "seq", [(i, ((i + 1) ^ 1) - 1) for i in range(1, count - 1)])
    weight_both = lax.ppermute(out_weight, "tp", swap)

    hbm = pl.BlockSpec(memory_space=pltpu.HBM)
    vmem = pl.BlockSpec(memory_space=pltpu.VMEM)
    attended_in, weight_own, residual_in = pl.pallas_call(
        functools.partial(attend_inner, frames),
        out_shape=[
            jax.ShapeDtypeStruct((inner, heads_width), jnp.bfloat16), halved,
            jax.ShapeDtypeStruct((inner, width), jnp.bfloat16),
        ],
        in_specs=[SMEM, SMEM, hbm, hbm, hbm, hbm, hbm],
        out_specs=[vmem, vmem, vmem],
        scratch_shapes=[
            pltpu.VMEM((pairs, 3, frames, LANES), jnp.bfloat16),
            pltpu.VMEM((inner // WIN, WIN, 3 * WIN), jnp.float32),
            pltpu.VMEM((2, frames, LANES), jnp.bfloat16),
            pltpu.VMEM((2, frames, 2 * LANES), jnp.bfloat16),
            pltpu.SemaphoreType.DMA((pairs, 3)),
            pltpu.SemaphoreType.DMA((2,)),
        ],
        compiler_params=params(42),
        cost_estimate=cost(0.001),
        name="attend_inner",
    )(record_starts, record_lengths, queries, attn_keys, attn_values, out_weight, residual)

    def projection(inside, operands, rows, microseconds, name):
        padded = -(-rows // LANES) * LANES
        shared = pltpu.VMEM((rows, LANES), jnp.float32)
        depth = heads_width if inside else 2 * heads_width
        return pl.pallas_call(
            functools.partial(project, inside),
            in_specs=[anywhere, anywhere, vmem] if inside else [anywhere] * 7,
            out_specs=[vmem, vmem],
            scratch_shapes=[pltpu.VMEM((rows, depth), jnp.bfloat16), pltpu.VMEM((depth, width), jnp.bfloat16)]
            + ([] if inside else [pltpu.VMEM((rows, width), jnp.bfloat16)])
            + [shared, shared, shared, pltpu.SemaphoreType.DMA((10,))],
            out_shape=[
                jax.ShapeDtypeStruct((rows, width), jnp.float32),
                jax.ShapeDtypeStruct((16, padded), jnp.float32),
            ],
            compiler_params=params(24),
            cost_estimate=cost(microseconds),
            name=name,
        )(*operands)

    other_in = lax.ppermute(attended_in, "tp", swap)
    base_in, weight_other = pl.pallas_call(
        project_own,
        in_specs=[vmem, vmem, vmem, hbm],
        out_specs=[vmem, vmem],
        out_shape=[jax.ShapeDtypeStruct((inner, width), jnp.float32), halved],
        scratch_shapes=[pltpu.SemaphoreType.DMA],
        compiler_params=params(8),
        cost_estimate=cost(10),
        name="project_own",
    )(attended_in, weight_own, residual_in, weight_both)
    hidden_in, stats_in = projection(True, [other_in, weight_other, base_in], inner, 0.001, "project_inner")
    other_stats_in = lax.ppermute(stats_in, "tp", swap)

    whole = lambda array: pl.BlockSpec(array.shape, lambda g: (0, 0))
    lane_block = lambda n, i=0: pl.BlockSpec((n, step), lambda g: (i, g))
    step = 2 * LANES
    gain = norm_gain.reshape(1, width)
    shared = lambda n: pltpu.VMEM(n + (LANES,), jnp.float32)
    kept = inner - 2 * EDGE
    result = jax.ShapeDtypeStruct((frames, width), jnp.bfloat16)
    partly = pl.pallas_call(
        functools.partial(norm_conv_inner, frames),
        grid=(width // step,),
        out_shape=result,
        in_specs=[SMEM, SMEM, lane_block(inner), whole(stats_in), whole(stats_in), lane_block(1), lane_block(KERNEL)],
        out_specs=anywhere,
        scratch_shapes=[
            shared((inner,)), shared((inner,)), shared((inner,)), shared((inner,)), shared((2, inner)), shared((2, 3, inner)),
            shared((2, 9, 8)),
            shared((3 * EDGE,)),
            pltpu.VMEM((2, kept, step), jnp.bfloat16),
            pltpu.SMEM((64,), jnp.int32),
            pltpu.SemaphoreType.DMA((2,)),
        ],
        compiler_params=params(16),
        cost_estimate=cost(0.001),
        name="norm_conv_inner",
    )(record_starts, record_lengths, hidden_in, stats_in, other_stats_in, gain, conv_weight)

    first, second, partly = lax.optimization_barrier((first, second, partly))
    wide = lambda n: pltpu.VMEM((2, n, heads_width), jnp.bfloat16)
    attended_end = pl.pallas_call(
        functools.partial(attend_ends, frames),
        out_shape=jax.ShapeDtypeStruct((ends, heads_width), jnp.bfloat16),
        in_specs=[SMEM, SMEM, hbm, hbm, hbm, anywhere, anywhere],
        out_specs=vmem,
        scratch_shapes=[
            pltpu.VMEM((2, REACH, SPAN), jnp.float32), wide(REACH), wide(SPAN), wide(SPAN), pltpu.SemaphoreType.DMA((12,)),
        ],
        compiler_params=params(16),
        cost_estimate=cost(5),
        name="attend_ends",
    )(record_starts, record_lengths, queries, attn_keys, attn_values, first, second)

    other_end = lax.ppermute(attended_end, "tp", swap)
    hidden_end, stats_end = projection(
        False, [attended_end, other_end, weight_own, weight_other, residual, first, second], ends, 4, "project_ends"
    )
    other_stats_end = lax.ppermute(stats_end, "tp", swap)

    more = 2 * EDGE
    rows = REACH + more
    return pl.pallas_call(
        functools.partial(norm_conv_ends, frames),
        grid=(width // step,),
        out_shape=result,
        in_specs=[
            SMEM, SMEM, lane_block(ends), lane_block(more), lane_block(more, inner // more - 1),
            whole(stats_end), whole(stats_end), whole(stats_in), whole(stats_in), lane_block(1), lane_block(KERNEL),
            anywhere,
        ],
        out_specs=anywhere,
        scratch_shapes=[
            shared((2, rows)), shared((2, rows)), shared((2, rows)), shared((2, rows)), shared((2, 2, rows)),
            shared((2, 2, rows)), shared((2, 2, 3, rows)), shared((2, 9, 8)), shared((3 * EDGE,)),
            pltpu.VMEM((2, 2, REACH, step), jnp.bfloat16),
            pltpu.SMEM((128,), jnp.int32),
            pltpu.SemaphoreType.DMA((2, 2)),
        ],
        input_output_aliases={11: 0},
        compiler_params=params(16),
        cost_estimate=cost(5),
        name="norm_conv_ends",
    )(
        record_starts, record_lengths, hidden_end, hidden_in, hidden_in, stats_end, other_stats_end, stats_in,
        other_stats_in, gain, conv_weight, partly,
    )


def solution(mesh):
    placed = (
        P(("grp", "seq"), "tp"),
        P(("grp", "seq"), "tp"),
        P(("grp", "seq"), "tp"),
        P("tp", None),
        P(("grp", "seq"), "tp"),
        P("tp"),
        P(None, "tp"),
        P("grp"),
        P("grp"),
    )
    return jax.shard_map(
        on_device, mesh=mesh, in_specs=placed, out_specs=P(("grp", "seq"), "tp"), check_vma=False
    )
```

```python
import functools

import jax
import jax.numpy as jnp
from jax import lax
from jax.experimental import pallas as pl
from jax.experimental.pallas import tpu as pltpu
from jax.sharding import PartitionSpec as P

D = 3072
HSIZE = 64
WIN = 128
KHALF = 15
REC = 8
KERNEL = 31
EDGE = 16
REACH = WIN + EDGE
SPAN = 512
LANES = 128
NEG = -1e30
SHARE = 3
EXP_SCALE = HSIZE ** (-0.5) * 1.4426950408889634
SMEM = pl.BlockSpec(memory_space=pltpu.SMEM)


def row_bounds(positions, starts_ref, lengths_ref):
    first = jnp.full(positions.shape, -1, jnp.int32)
    last = jnp.full(positions.shape, -2, jnp.int32)
    for r in range(REC):
        start = starts_ref[r]
        end = start + lengths_ref[r]
        inside = (positions >= start) & (positions < end)
        first = jnp.where(inside, start, first)
        last = jnp.where(inside, end - 1, last)
    return first, last


def as_column(row):
    return jnp.transpose(jnp.broadcast_to(row, (LANES, LANES)))


def band_bias(base, rows, key_base, keys, starts_ref, lengths_ref, store):
    for top in range(0, rows, LANES):
        count = min(LANES, rows - top)
        positions = base + top + lax.broadcasted_iota(jnp.int32, (1, LANES), 1)
        first, last = row_bounds(positions, starts_ref, lengths_ref)
        inside = first >= 0
        low = jnp.where(inside, jnp.maximum(first, positions - WIN), 0)
        high = jnp.where(inside, jnp.minimum(last, positions + WIN), -1)
        low = as_column(low.astype(jnp.float32))
        high = as_column(high.astype(jnp.float32))
        for left in range(0, keys, LANES):
            key_at = (key_base + left + lax.broadcasted_iota(jnp.int32, (LANES, LANES), 1)).astype(jnp.float32)
            bias = jnp.where((key_at >= low) & (key_at <= high), jnp.float32(0.0), jnp.float32(NEG))
            store(top, count, left, bias[:count])


def head_pair(query, keys, values, bias):
    span = bias.shape[1]
    scores = lax.dot_general(query, keys, (((1,), (1,)), ((), ())), preferred_element_type=jnp.float32)
    weights = []
    for h in range(2):
        part = scores[:, h * span : (h + 1) * span] + bias
        row_max = jnp.max(part, axis=1, keepdims=True)
        weights.append(jnp.exp2((part - row_max) * EXP_SCALE).astype(jnp.bfloat16))
    mixed = jnp.dot(jnp.concatenate(weights, axis=1), values, preferred_element_type=jnp.float32)
    return jnp.where(bias_any(bias), mixed[:, :LANES] / mixed[:, LANES:], 0.0).astype(jnp.bfloat16)


def bias_any(bias):
    return jnp.max(bias, axis=1, keepdims=True) > NEG / 2


def split_heads(array):
    left = lax.broadcasted_iota(jnp.int32, array.shape, 1) < HSIZE
    nothing = jnp.zeros_like(array)
    return jnp.where(left, array, nothing), jnp.where(left, nothing, array)


def start_all(copies):
    for copy in copies:
        copy.start()
    return copies


def wait_all(copies):
    for copy in copies:
        copy.wait()


def attend_inner(
    frames, starts_ref, lengths_ref, q_hbm, k_hbm, v_hbm, w_hbm, r_hbm, o_ref, w_own_ref, r_in_ref,
    columns, bias, keys, values, sems, more_sems
):
    blocks = frames // WIN - 2
    span = 3 * WIN
    pairs = q_hbm.shape[1] // LANES
    anchor = lax.axis_index("seq") * frames

    def fetch(p):
        lanes = pl.ds(p * LANES, LANES)
        return [
            pltpu.make_async_copy(ref.at[:, lanes], columns.at[p, n], sems.at[p, n])
            for n, ref in enumerate((q_hbm, k_hbm, v_hbm))
        ]

    for p in range(pairs):
        start_all(fetch(p))
    width = w_own_ref.shape[1]
    mine = pl.multiple_of(lax.axis_index("tp") * width, LANES)
    later = start_all([
        pltpu.make_async_copy(w_hbm.at[:, pl.ds(mine, width)], w_own_ref, more_sems.at[0]),
        pltpu.make_async_copy(r_hbm.at[pl.ds(WIN, blocks * WIN), :], r_in_ref, more_sems.at[1]),
    ])
    values[0, :, LANES:], values[1, :, LANES:] = split_heads(jnp.ones((frames, LANES), jnp.bfloat16))
    for i in range(blocks):
        def store(top, count, left, value):
            bias[i, top : top + count, left : left + LANES] = value

        band_bias(anchor + (i + 1) * WIN, WIN, anchor + i * WIN, span, starts_ref, lengths_ref, store)

    def one_pair(p, carry):
        lanes = pl.ds(pl.multiple_of(p * LANES, LANES), LANES)
        for n, ref in enumerate((q_hbm, k_hbm, v_hbm)):
            pltpu.make_async_copy(ref.at[:, lanes], columns.at[p, n], sems.at[p, n]).wait()
        keys[0], keys[1] = split_heads(columns[p, 1])
        values[0, :, :LANES], values[1, :, :LANES] = split_heads(columns[p, 2])
        for i in range(blocks):
            window = slice(i * WIN, i * WIN + span)
            o_ref[i * WIN : (i + 1) * WIN, lanes] = head_pair(
                columns[p, 0, (i + 1) * WIN : (i + 2) * WIN, :],
                jnp.concatenate([keys[0, window, :], keys[1, window, :]], axis=0),
                jnp.concatenate([values[0, window, :], values[1, window, :]], axis=0),
                bias[i],
            )
        return carry

    lax.fori_loop(0, pairs, one_pair, 0)
    wait_all(later)


def halo_side():
    return 1 - lax.axis_index("seq") % 2


def attend_ends(
    frames, starts_ref, lengths_ref, q_hbm, k_hbm, v_hbm, first_hbm, second_hbm, o_ref, bias, query, keys, values, sems
):
    anchor = lax.axis_index("seq") * frames
    own = SPAN - REACH
    pairs = q_hbm.shape[1] // LANES
    side = halo_side()
    copies = []

    def move(source, target):
        copies.append(pltpu.make_async_copy(source, target, sems.at[len(copies)]))

    for target, ref, at, rows, mine in (
        (query, q_hbm, 2 * EDGE, EDGE, WIN), (keys, k_hbm, 3 * EDGE, REACH, own), (values, v_hbm, 3 * EDGE + REACH, REACH, own)
    ):
        move(ref.at[pl.ds(0, mine), :], target.at[0, pl.ds(rows, mine), :])
        move(ref.at[pl.ds(frames - mine, mine), :], target.at[1, pl.ds(0, mine), :])
        for halo, which in ((first_hbm, side), (second_hbm, 1 - side)):
            top = pl.multiple_of(which * mine, EDGE)
            move(halo.at[pl.ds(at, rows), :], target.at[which, pl.ds(top, rows), :])
    start_all(copies)
    for i, (base, key_base) in enumerate(((-EDGE, -REACH), (frames - WIN, frames - own))):
        def store(top, count, left, value):
            bias[i, top : top + count, left : left + LANES] = value

        band_bias(anchor + base, REACH, anchor + key_base, SPAN, starts_ref, lengths_ref, store)
    wait_all(copies)
    ones = split_heads(jnp.ones((SPAN, LANES), jnp.bfloat16))
    for p in range(pairs):
        lanes = slice(p * LANES, (p + 1) * LANES)
        for i in range(2):
            sides = [jnp.concatenate([v, one], axis=1) for v, one in zip(split_heads(values[i, :, lanes]), ones)]
            o_ref[i * REACH : (i + 1) * REACH, lanes] = head_pair(
                query[i, :, lanes],
                jnp.concatenate(split_heads(keys[i, :, lanes]), axis=0),
                jnp.concatenate(sides, axis=0),
                bias[i],
            )


def pack_edges(frames, q_ref, k_ref, v_ref, r_ref, first_ref, second_ref, sems):
    half = q_ref.shape[1]
    odd = lax.axis_index("seq") % 2
    copies = []
    for i, out in enumerate((first_ref, second_ref)):
        bottom = (1 - odd) if i == 0 else odd

        def rows(ref, n, left=0):
            return ref.at[pl.ds(pl.multiple_of(bottom * (frames - n), EDGE), n), pl.ds(left, half)]

        moves = [
            (rows(r_ref, EDGE), 0, EDGE),
            (rows(r_ref, EDGE, half), EDGE, EDGE),
            (rows(q_ref, EDGE), 2 * EDGE, EDGE),
            (rows(k_ref, REACH), 3 * EDGE, REACH),
            (rows(v_ref, REACH), 3 * EDGE + REACH, REACH),
        ]
        for n, (source, at, count) in enumerate(moves):
            copies.append(pltpu.make_async_copy(source, out.at[pl.ds(at, count), :], sems.at[i, n]))
    wait_all(start_all(copies))


def project_own(own_ref, w_ref, r_ref, more_hbm, o_ref, more_ref, sem):
    step = 256
    width = more_ref.shape[1]
    left = pl.multiple_of(lax.axis_index("tp") * width, LANES)
    later = pltpu.make_async_copy(more_hbm.at[:, pl.ds(left, width)], more_ref, sem)
    later.start()
    for left in range(0, o_ref.shape[1], step):
        cols = slice(left, left + step)
        part = jnp.dot(own_ref[...], w_ref[:, cols], preferred_element_type=jnp.float32)
        o_ref[:, cols] = part + r_ref[:, cols].astype(jnp.float32)
    later.wait()


def project(inner, *refs):
    if inner:
        other_hbm, w_other_hbm, base, h_ref, stats_ref, left, right, shift, first, second, sems = refs
    else:
        (own_hbm, other_hbm, w_own_hbm, w_other_hbm, r_hbm, first_hbm, second_hbm,
         h_ref, stats_ref, left, right, base, shift, first, second, sems) = refs
    rows, width = h_ref.shape
    half = other_hbm.shape[1]
    step = 256
    copies = []

    def move(source, target):
        copies.append(pltpu.make_async_copy(source, target, sems.at[len(copies)]))

    at = left.shape[1] - half
    move(other_hbm, left.at[:, pl.ds(at, half)])
    move(w_other_hbm, right.at[pl.ds(at, half), :])
    if not inner:
        move(own_hbm, left.at[:, pl.ds(0, half)])
        move(w_own_hbm, right.at[pl.ds(0, half), :])
        frames = r_hbm.shape[0]
        move(r_hbm.at[pl.ds(0, WIN), :], base.at[pl.ds(EDGE, WIN), :])
        move(r_hbm.at[pl.ds(frames - WIN, WIN), :], base.at[pl.ds(REACH, WIN), :])
        side = halo_side()
        for halo, which in ((first_hbm, side), (second_hbm, 1 - side)):
            target = pl.ds(pl.multiple_of(which * (REACH + WIN), EDGE), EDGE)
            for n in range(2):
                move(halo.at[pl.ds(n * EDGE, EDGE), :], base.at[target, pl.ds(n * half, half)])
    wait_all(start_all(copies))

    def gather(j):
        first_sum, second_sum = first[...], second[...]
        for l in range(j * step, (j + 1) * step, LANES):
            off = h_ref[:, l : l + LANES] - shift[...]
            first_sum = first_sum + off
            second_sum = second_sum + off * off
        first[...] = first_sum
        second[...] = second_sum

    first[...] = jnp.zeros_like(first)
    second[...] = jnp.zeros_like(second)
    for j in range(width // step):
        cols = slice(j * step, (j + 1) * step)
        part = jnp.dot(left[...], right[:, cols], preferred_element_type=jnp.float32)
        h_ref[:, cols] = part + base[:, cols].astype(jnp.float32)
        if j == 0:
            mean = jnp.sum(h_ref[:, cols], axis=1, keepdims=True) * (1.0 / step)
            shift[...] = jnp.broadcast_to(mean, (rows, LANES))
        else:
            gather(j - 1)
    gather(width // step - 1)
    moved = jnp.sum(first[...], axis=1, keepdims=True) * (1.0 / width)
    mean = shift[...] + moved
    square = jnp.sum(second[...], axis=1, keepdims=True) - moved * moved * float(width)
    for top in range(0, rows, LANES):
        count = min(LANES, rows - top)
        for k, column in enumerate((mean, jnp.broadcast_to(square, (rows, LANES)))):
            tile = column[top : top + count]
            if count < LANES:
                tile = jnp.concatenate([tile, jnp.zeros((LANES - count, LANES), jnp.float32)], axis=0)
            stats_ref[8 * k : 8 * k + 8, top : top + LANES] = jnp.transpose(tile)[:8, :]


def recording_of(base, starts_ref, lengths_ref):
    positions = base + lax.broadcasted_iota(jnp.int32, (1, LANES), 1)
    index = jnp.zeros((1, LANES), jnp.int32) - 1
    for r in range(REC):
        start = starts_ref[r]
        inside = (positions >= start) & (positions < start + lengths_ref[r])
        index = jnp.where(inside, r, index)
    return index


def stat_columns(base, own, other, width, starts_ref, lengths_ref):
    inside = recording_of(base, starts_ref, lengths_ref) >= 0
    gap = own[0:1, :] - other[0:1, :]
    middle = 0.5 * (own[0:1, :] + other[0:1, :])
    var = (own[8:9, :] + other[8:9, :] + gap * gap * (width * 0.25)) * (1.0 / width)
    inverse = jnp.where(inside, lax.rsqrt(var + 1e-5), 0.0)
    deviation = as_column(inverse)
    return as_column(middle), deviation, jnp.where(deviation > 0, 0.5, 0.0)


def parity_column(base, starts_ref, lengths_ref):
    index = recording_of(base, starts_ref, lengths_ref)
    return as_column(jnp.where(index >= 0, (index % 2).astype(jnp.float32), -1.0))


def mark_mixed(base, chunks, flags, at, starts_ref, lengths_ref):
    flags[at] = jnp.int32(0)
    for r in range(REC - 1):
        end, start = starts_ref[r] + lengths_ref[r], starts_ref[r + 1]
        low = jnp.maximum((end - KHALF - base) >> 4, 0)
        high = jnp.minimum((start + KHALF - base + EDGE - 1) >> 4, chunks)

        @pl.when(start - end < KHALF)
        def _():
            def add(c, carry):
                known = flags[at]
                flags[at + 1 + known] = c
                flags[at] = known + 1
                return carry

            lax.fori_loop(low, high, add, 0)


def convolve(load, w_ref):
    acc = load(0) * w_ref[0:1, :]
    for tap in range(1, KERNEL):
        acc = acc + load(tap) * w_ref[tap : tap + 1, :]
    return acc


def differences(x_ref, diffs):
    rows = x_ref.shape[0]
    x = x_ref[...]
    near = x[: rows - 8] - x[8:]
    diffs[0, : rows - 8, :] = near
    diffs[1, : rows - 16, :] = x[: rows - 16] - x[16:]
    diffs[2, : rows - 24, :] = near[: rows - 24] - near[16:]


def tap_sums(w_ref, wq):
    padded = jnp.concatenate([jnp.zeros((1, LANES), jnp.float32), w_ref[...]], axis=0)
    w0, w1, w2, w3 = (padded[8 * j : 8 * j + 8] for j in range(4))
    for n, value in enumerate((w0, w0 + w1, -w1, w0 + w2, w0 + w1 + w2 + w3, -(w1 + w3), -w2, -(w2 + w3), w3)):
        wq[n] = value


def conv_groups(x_ref, diffs, wq, ats):
    sources = (
        (diffs.at[2], 0), (diffs.at[1], 8), (diffs.at[2], 8),
        (diffs.at[0], 16), (x_ref, 24), (diffs.at[0], 24),
        (diffs.at[2], 16), (diffs.at[1], 24), (diffs.at[2], 24),
    )
    sums = [[None] * 9 for _ in ats]
    for s in range(8):
        for n, (ref, off) in enumerate(sources):
            weight = jnp.broadcast_to(wq[n, s : s + 1, :], (8, LANES))
            for group, at in zip(sums, ats):
                first = at - EDGE + s + off
                term = ref[first : first + 8, :] * weight
                group[n] = term if group[n] is None else group[n] + term
    results = []
    for t in sums:
        a0, a1 = t[1] + t[0], t[1] + t[2]
        p0, p1 = t[4] + t[3], t[4] + t[5]
        c0, c1 = t[7] + t[6], t[7] + t[8]
        results.append(jnp.concatenate([a0 + p0, a1 + p1, p0 + c0, p1 + c1], axis=0))
    return results


def silu_add(hidden, half):
    return (hidden + (half + half * jnp.tanh(half))).astype(jnp.bfloat16)


def conv_rows(rows, hidden, normed, parity, halves, diffs, wq, masked, flags, flag_at, w_ref, out):
    differences(normed, diffs)
    tap_sums(w_ref, wq)
    group = 2 * EDGE
    tops = list(range(0, rows - group, group)) + [rows - group]
    for start in range(0, len(tops), SHARE):
        some = tops[start : start + SHARE]
        for top, conv_sum in zip(some, conv_groups(normed, diffs, wq, [top + EDGE for top in some])):
            at = top + EDGE
            here = slice(at, at + group)
            out[top : top + group, :] = silu_add(hidden[here, :], conv_sum * halves[here, :])

    def again(c, carry):
        top = pl.multiple_of(flags[flag_at + 1 + c] * EDGE, EDGE)
        around, here = pl.ds(top, 3 * EDGE), pl.ds(top + EDGE, EDGE)
        conv_sum = jnp.zeros((EDGE, LANES), jnp.float32)
        for side in range(2):
            masked[...] = jnp.where(parity[around, :] == side, normed[around, :], 0.0)
            first = EDGE - KHALF
            part = convolve(lambda tap: masked[first + tap : first + tap + EDGE, :], w_ref)
            conv_sum = jnp.where(parity[here, :] == side, part, conv_sum)
        out[pl.ds(top, EDGE), :] = silu_add(hidden[here, :], conv_sum * 0.5)
        return carry

    lax.fori_loop(0, flags[flag_at], again, 0)


def norm_conv_inner(
    frames, starts_ref, lengths_ref, h_ref, own_ref, other_ref, gain_ref, w_ref, o_ref,
    mean, scale, parity, halves, normed, diffs, wq, masked, out, flags, sems,
):
    step, steps = pl.program_id(0), pl.num_programs(0)
    rows, wide = h_ref.shape
    kept = rows - 2 * EDGE
    base = lax.axis_index("seq") * frames + WIN

    @pl.when(step == 0)
    def _():
        width = 2.0 * wide * steps
        mark_mixed(base + EDGE, kept // EDGE, flags, 0, starts_ref, lengths_ref)
        for top in range(0, rows, LANES):
            here = slice(top, top + LANES)
            mean[here, :], scale[here, :], halves[here, :] = stat_columns(
                base + top, own_ref[:, here], other_ref[:, here], width, starts_ref, lengths_ref
            )

        @pl.when(flags[0] > 0)
        def _():
            for top in range(0, rows, LANES):
                parity[top : top + LANES, :] = parity_column(base + top, starts_ref, lengths_ref)

    slot = step % 2

    def copy(at, which):
        lanes = pl.ds(pl.multiple_of(at * wide, LANES), wide)
        return pltpu.make_async_copy(out.at[which], o_ref.at[pl.ds(WIN + EDGE, kept), lanes], sems.at[which])

    @pl.when(step >= 2)
    def _():
        copy(step - 2, slot).wait()

    for u in range(wide // LANES):
        lanes = slice(u * LANES, (u + 1) * LANES)
        value = (h_ref[:, lanes] - mean[...]) * scale[...] * gain_ref[:, lanes]
        normed[u] = value.astype(jnp.bfloat16).astype(jnp.float32)
        conv_rows(
            kept, h_ref.at[:, lanes], normed.at[u], parity, halves, diffs.at[u], wq.at[u], masked, flags, 0,
            w_ref.at[:, lanes], out.at[slot, :, lanes],
        )
    copy(step, slot).start()

    @pl.when(step == steps - 1)
    def _():
        copy(step - 1, 1 - slot).wait()
        copy(step, slot).wait()


def norm_conv_ends(
    frames, starts_ref, lengths_ref, h_end_ref, h_low_ref, h_high_ref, s_end_ref, t_end_ref, s_in_ref, t_in_ref,
    gain_ref, w_ref, done_ref, o_ref, mean, scale, parity, halves, hidden, normed, diffs, wq, masked, out, flags, sems,
):
    step, steps = pl.program_id(0), pl.num_programs(0)
    inner = frames - 2 * WIN
    anchor = lax.axis_index("seq") * frames
    more = 2 * EDGE
    rows = REACH + more
    wide = h_end_ref.shape[1]

    @pl.when(step == 0)
    def _():
        width = 2.0 * wide * steps
        for i in range(2):
            mark_mixed(anchor + i * (frames - REACH), REACH // EDGE, flags, i * 64, starts_ref, lengths_ref)

        def joined(ends, ins, i):
            if i == 0:
                return jnp.concatenate([ends[:, :REACH], ins[:, : 2 * LANES - REACH]], axis=1)
            return jnp.concatenate([ins[:, inner - more :], ends[:, REACH : REACH + 2 * LANES - more]], axis=1)

        for i, first in enumerate((anchor - EDGE, anchor + frames - WIN - more)):
            own, other = joined(s_end_ref, s_in_ref, i), joined(t_end_ref, t_in_ref, i)
            for top, count in ((0, LANES), (LANES, rows - LANES)):
                here, lanes = slice(top, top + count), slice(top, top + LANES)
                values = stat_columns(first + top, own[:, lanes], other[:, lanes], width, starts_ref, lengths_ref)
                for ref, value in zip((mean, scale, halves), values):
                    ref[i, here, :] = value[:count]

                @pl.when(flags[0] + flags[64] > 0)
                def _():
                    parity[i, here, :] = parity_column(first + top, starts_ref, lengths_ref)[:count]

    slot = step % 2

    def copies(at, which):
        lanes = pl.ds(pl.multiple_of(at * wide, LANES), wide)
        return [
            pltpu.make_async_copy(
                out.at[which, i], o_ref.at[pl.ds(i * (frames - REACH), REACH), lanes], sems.at[which, i]
            )
            for i in range(2)
        ]

    @pl.when(step >= 2)
    def _():
        for copy in copies(step - 2, slot):
            copy.wait()

    for u in range(wide // LANES):
        lanes = slice(u * LANES, (u + 1) * LANES)
        hidden[u, 0, :REACH, :] = h_end_ref[:REACH, lanes]
        hidden[u, 0, REACH:, :] = h_low_ref[:, lanes]
        hidden[u, 1, :more, :] = h_high_ref[:, lanes]
        hidden[u, 1, more:, :] = h_end_ref[REACH:, lanes]
        for i in range(2):
            value = (hidden[u, i] - mean[i]) * scale[i] * gain_ref[:, lanes]
            normed[u, i] = value.astype(jnp.bfloat16).astype(jnp.float32)
            conv_rows(
                REACH, hidden.at[u, i], normed.at[u, i], parity.at[i], halves.at[i], diffs.at[u, i], wq.at[u], masked,
                flags, i * 64, w_ref.at[:, lanes], out.at[slot, i, :, lanes],
            )
    for copy in copies(step, slot):
        copy.start()

    @pl.when(step == steps - 1)
    def _():
        for copy in copies(step - 1, 1 - slot) + copies(step, slot):
            copy.wait()


def cost(microseconds):
    return pl.CostEstimate(flops=int(microseconds * 4e8), bytes_accessed=1000, transcendentals=0)


def params(mebibytes):
    return pltpu.CompilerParams(vmem_limit_bytes=mebibytes * 2**20)


def on_device(
    queries, attn_keys, attn_values, out_weight, residual, norm_gain, conv_weight, record_starts, record_lengths
):
    frames, heads_width = queries.shape
    width = residual.shape[1]
    pairs = heads_width // LANES
    inner = frames - 2 * WIN
    ends = 2 * REACH
    count = lax.axis_size("seq")
    swap = [(0, 1), (1, 0)]
    anywhere = pl.BlockSpec(memory_space=pl.ANY)

    edges = jax.ShapeDtypeStruct((3 * EDGE + 2 * REACH, heads_width), jnp.bfloat16)
    halved = jax.ShapeDtypeStruct((heads_width, width), jnp.bfloat16)
    first_edge, second_edge = pl.pallas_call(
        functools.partial(pack_edges, frames),
        out_shape=[edges, edges],
        in_specs=[pl.BlockSpec(memory_space=pltpu.HBM)] * 4,
        out_specs=[pl.BlockSpec(memory_space=pltpu.VMEM)] * 2,
        scratch_shapes=[pltpu.SemaphoreType.DMA((2, 5))],
        compiler_params=params(52),
        name="pack_edges",
    )(queries, attn_keys, attn_values, residual)
    first_edge, second_edge, queries = lax.optimization_barrier((first_edge, second_edge, queries))
    first = lax.ppermute(first_edge, "seq", [(i, i ^ 1) for i in range(count)])
    second = lax.ppermute(second_edge, "seq", [(i, ((i + 1) ^ 1) - 1) for i in range(1, count - 1)])
    weight_both = lax.ppermute(out_weight, "tp", swap)

    hbm = pl.BlockSpec(memory_space=pltpu.HBM)
    vmem = pl.BlockSpec(memory_space=pltpu.VMEM)
    attended_in, weight_own, residual_in = pl.pallas_call(
        functools.partial(attend_inner, frames),
        out_shape=[
            jax.ShapeDtypeStruct((inner, heads_width), jnp.bfloat16), halved,
            jax.ShapeDtypeStruct((inner, width), jnp.bfloat16),
        ],
        in_specs=[SMEM, SMEM, hbm, hbm, hbm, hbm, hbm],
        out_specs=[vmem, vmem, vmem],
        scratch_shapes=[
            pltpu.VMEM((pairs, 3, frames, LANES), jnp.bfloat16),
            pltpu.VMEM((inner // WIN, WIN, 3 * WIN), jnp.float32),
            pltpu.VMEM((2, frames, LANES), jnp.bfloat16),
            pltpu.VMEM((2, frames, 2 * LANES), jnp.bfloat16),
            pltpu.SemaphoreType.DMA((pairs, 3)),
            pltpu.SemaphoreType.DMA((2,)),
        ],
        compiler_params=params(42),
        cost_estimate=cost(0.001),
        name="attend_inner",
    )(record_starts, record_lengths, queries, attn_keys, attn_values, out_weight, residual)

    def projection(inside, operands, rows, microseconds, name):
        padded = -(-rows // LANES) * LANES
        shared = pltpu.VMEM((rows, LANES), jnp.float32)
        depth = heads_width if inside else 2 * heads_width
        return pl.pallas_call(
            functools.partial(project, inside),
            in_specs=[anywhere, anywhere, vmem] if inside else [anywhere] * 7,
            out_specs=[vmem, vmem],
            scratch_shapes=[pltpu.VMEM((rows, depth), jnp.bfloat16), pltpu.VMEM((depth, width), jnp.bfloat16)]
            + ([] if inside else [pltpu.VMEM((rows, width), jnp.bfloat16)])
            + [shared, shared, shared, pltpu.SemaphoreType.DMA((10,))],
            out_shape=[
                jax.ShapeDtypeStruct((rows, width), jnp.float32),
                jax.ShapeDtypeStruct((16, padded), jnp.float32),
            ],
            compiler_params=params(24),
            cost_estimate=cost(microseconds),
            name=name,
        )(*operands)

    other_in = lax.ppermute(attended_in, "tp", swap)
    base_in, weight_other = pl.pallas_call(
        project_own,
        in_specs=[vmem, vmem, vmem, hbm],
        out_specs=[vmem, vmem],
        out_shape=[jax.ShapeDtypeStruct((inner, width), jnp.float32), halved],
        scratch_shapes=[pltpu.SemaphoreType.DMA],
        compiler_params=params(8),
        cost_estimate=cost(10),
        name="project_own",
    )(attended_in, weight_own, residual_in, weight_both)
    hidden_in, stats_in = projection(True, [other_in, weight_other, base_in], inner, 0.001, "project_inner")
    other_stats_in = lax.ppermute(stats_in, "tp", swap)

    whole = lambda array: pl.BlockSpec(array.shape, lambda g: (0, 0))
    lane_block = lambda n, i=0: pl.BlockSpec((n, step), lambda g: (i, g))
    step = 2 * LANES
    gain = norm_gain.reshape(1, width)
    shared = lambda n: pltpu.VMEM(n + (LANES,), jnp.float32)
    kept = inner - 2 * EDGE
    result = jax.ShapeDtypeStruct((frames, width), jnp.bfloat16)
    partly = pl.pallas_call(
        functools.partial(norm_conv_inner, frames),
        grid=(width // step,),
        out_shape=result,
        in_specs=[SMEM, SMEM, lane_block(inner), whole(stats_in), whole(stats_in), lane_block(1), lane_block(KERNEL)],
        out_specs=anywhere,
        scratch_shapes=[
            shared((inner,)), shared((inner,)), shared((inner,)), shared((inner,)), shared((2, inner)), shared((2, 3, inner)),
            shared((2, 9, 8)),
            shared((3 * EDGE,)),
            pltpu.VMEM((2, kept, step), jnp.bfloat16),
            pltpu.SMEM((64,), jnp.int32),
            pltpu.SemaphoreType.DMA((2,)),
        ],
        compiler_params=params(16),
        cost_estimate=cost(0.001),
        name="norm_conv_inner",
    )(record_starts, record_lengths, hidden_in, stats_in, other_stats_in, gain, conv_weight)

    first, second, partly = lax.optimization_barrier((first, second, partly))
    wide = lambda n: pltpu.VMEM((2, n, heads_width), jnp.bfloat16)
    attended_end = pl.pallas_call(
        functools.partial(attend_ends, frames),
        out_shape=jax.ShapeDtypeStruct((ends, heads_width), jnp.bfloat16),
        in_specs=[SMEM, SMEM, hbm, hbm, hbm, anywhere, anywhere],
        out_specs=vmem,
        scratch_shapes=[
            pltpu.VMEM((2, REACH, SPAN), jnp.float32), wide(REACH), wide(SPAN), wide(SPAN), pltpu.SemaphoreType.DMA((12,)),
        ],
        compiler_params=params(16),
        cost_estimate=cost(5),
        name="attend_ends",
    )(record_starts, record_lengths, queries, attn_keys, attn_values, first, second)

    other_end = lax.ppermute(attended_end, "tp", swap)
    hidden_end, stats_end = projection(
        False, [attended_end, other_end, weight_own, weight_other, residual, first, second], ends, 4, "project_ends"
    )
    other_stats_end = lax.ppermute(stats_end, "tp", swap)

    more = 2 * EDGE
    rows = REACH + more
    return pl.pallas_call(
        functools.partial(norm_conv_ends, frames),
        grid=(width // step,),
        out_shape=result,
        in_specs=[
            SMEM, SMEM, lane_block(ends), lane_block(more), lane_block(more, inner // more - 1),
            whole(stats_end), whole(stats_end), whole(stats_in), whole(stats_in), lane_block(1), lane_block(KERNEL),
            anywhere,
        ],
        out_specs=anywhere,
        scratch_shapes=[
            shared((2, rows)), shared((2, rows)), shared((2, rows)), shared((2, rows)), shared((2, 2, rows)),
            shared((2, 2, rows)), shared((2, 2, 3, rows)), shared((2, 9, 8)), shared((3 * EDGE,)),
            pltpu.VMEM((2, 2, REACH, step), jnp.bfloat16),
            pltpu.SMEM((128,), jnp.int32),
            pltpu.SemaphoreType.DMA((2, 2)),
        ],
        input_output_aliases={11: 0},
        compiler_params=params(16),
        cost_estimate=cost(5),
        name="norm_conv_ends",
    )(
        record_starts, record_lengths, hidden_end, hidden_in, hidden_in, stats_end, other_stats_end, stats_in,
        other_stats_in, gain, conv_weight, partly,
    )


def solution(mesh):
    placed = (
        P(("grp", "seq"), "tp"),
        P(("grp", "seq"), "tp"),
        P(("grp", "seq"), "tp"),
        P("tp", None),
        P(("grp", "seq"), "tp"),
        P("tp"),
        P(None, "tp"),
        P("grp"),
        P("grp"),
    )
    return jax.shard_map(
        on_device, mesh=mesh, in_specs=placed, out_specs=P(("grp", "seq"), "tp"), check_vma=False
    )
```
